128 devices in a mesh: dp: 4 (over x_hi, core), tensor: 32 (over x_lo, y, z).
Axes of the slice: x: 4 (x_hi: 2, x_lo: 2; x = x_hi * 2 + x_lo), y: 4, z: 4, core: 2. Of those that a mesh axis runs over, the one named last changes fastest.
Arguments:
- teacher_hidden: bfloat16 [5120, 24576], P('dp', 'tensor'), may hold values from -40 to 40, as said below
- teacher_down: bfloat16 [24576, 3072], P('tensor'), may hold values from -0.0390625 to 0.0390625
- teacher_gain: float32 [3072], replicated, may hold values from 0.5 to 1.5
- student_stream: bfloat16 [5120, 1024], P(('dp', 'tensor')), may hold values from -45 to 45
- contexts: bfloat16 [2, 5120, 1024], P(None, ('dp', 'tensor')), may hold values from -6 to 6
- proj_weight: bfloat16 [2, 1024, 1024], P(None, 'tensor'), may hold values from -0.1875 to 0.1875
- student_gain: float32 [1024], replicated, may hold values from 0.5 to 1.5
- head_weight: bfloat16 [1024, 3072], P(None, 'tensor'), may hold values from -0.1875 to 0.1875
Outputs:
- head_grad: float32 [1024, 3072], P(None, 'tensor')
- proj_grad: float32 [2, 1024, 1024], P(None, 'tensor')
The draws below stay inside these ranges and needn't reach their ends.
Inputs may be any that keep to these rules, and one draw needn't show every extreme that they name: `teacher_hidden`: teacher activations of every row.
All inputs are finite; a program needn't handle non-finite values.
Results may differ from the reference program's by a relative error of at most 0.0085.
Values may be sent and summed in bfloat16 or wider, within the bound.
A program may use at most 128 MiB of HBM per device.

```python
import math
import jax
import jax.numpy as jnp
from jax import lax

FF_T = 24576
FEAT = 3072
D_S = 1024
BLOCKS = 2
TOKENS = 5120


def draw_teacher_hidden(key, part):
    key = jax.random.fold_in(key, 7)
    value_key, scale_key = jax.random.split(key)
    values_raw = jnp.clip(jax.random.normal(value_key, (TOKENS, FF_T), jnp.float32), -4.0, 4.0)
    spread = math.log(10.0)
    row_scale = jnp.exp(jax.random.uniform(scale_key, (TOKENS, 1), jnp.float32, 0.0, spread))
    return (values_raw * row_scale).astype(jnp.bfloat16)


def draw_student_stream(key, part):
    key = jax.random.fold_in(key, 19)
    value_key, row_key, col_key = jax.random.split(key, 3)
    values_raw = jnp.clip(jax.random.normal(value_key, (TOKENS, D_S), jnp.float32), -4.0, 4.0)
    lowest = math.log(0.3)
    row_scale = jnp.exp(jax.random.uniform(row_key, (TOKENS, 1), jnp.float32, lowest, -lowest))
    col_scale = jnp.exp(jax.random.uniform(col_key, (1, D_S), jnp.float32, lowest, -lowest))
    return (values_raw * row_scale * col_scale).astype(jnp.bfloat16)


def levels(rng, dims, cuts, low, high):
    level, own = 1.0, jax.random.fold_in(rng, 6)
    for position, blocks in cuts:
        steps = jnp.exp(jax.random.uniform(jax.random.fold_in(own, position), (blocks,), jnp.float32, low / len(cuts), high / len(cuts)))
        level = level * jnp.repeat(steps, dims[position] // blocks).reshape([-1 if axis == position else 1 for axis in range(len(dims))])
    return level


def scatter_about(own_key, shape, scale, reach, pieces=(), dtype=jnp.bfloat16):
    array = scale * jax.random.normal(own_key, shape, jnp.float32)
    if pieces:
        array = array * levels(own_key, shape, pieces, -0.22, 0.18)
    return jnp.clip(array, -reach, reach).astype(dtype)


def setup_inputs(seed: int = 0) -> dict:
    arg_keys = jax.random.split(jax.random.key(seed), 9)
    return {
        "teacher_hidden": draw_teacher_hidden(jax.random.fold_in(arg_keys[8], 71), 0),
        "teacher_down": scatter_about(arg_keys[1], (FF_T, FEAT), FF_T ** -0.5, 0.0390625, ((0, 32),)),
        "teacher_gain": jnp.clip(jax.random.uniform(arg_keys[2], (FEAT,), jnp.float32, 0.5, 1.5), 0.5, 1.5),
        "student_stream": draw_student_stream(jax.random.fold_in(arg_keys[8], 71), 0),
        "contexts": scatter_about(arg_keys[4], (BLOCKS, TOKENS, D_S), 1.0, 6.0, ((1, 128),)),
        "proj_weight": scatter_about(arg_keys[5], (BLOCKS, D_S, D_S), D_S ** -0.5, 0.1875, ((1, 32),)),
        "student_gain": jnp.clip(jax.random.uniform(arg_keys[6], (D_S,), jnp.float32, 0.5, 1.5), 0.5, 1.5),
        "head_weight": scatter_about(arg_keys[7], (D_S, FEAT), D_S ** -0.5, 0.1875, ((1, 32),)),
    }


epsilon = 1e-06

def normalize(values, gain):
    mean_value = lax.optimization_barrier(jnp.mean(values, axis=-1, keepdims=True))
    centered = values - mean_value
    variance = lax.optimization_barrier(jnp.mean(centered * centered, axis=-1, keepdims=True))
    inv_std = lax.rsqrt(variance + epsilon)
    normed = centered * inv_std
    return (normed * gain, normed, inv_std)

def normalize_back(grad_out, gain, normed, inv_std):
    weighted = grad_out * gain
    first_mean = lax.optimization_barrier(jnp.mean(weighted, axis=-1, keepdims=True))
    second_mean = lax.optimization_barrier(jnp.mean(weighted * normed, axis=-1, keepdims=True))
    return inv_std * (weighted - first_mean - normed * second_mean)

def reference(teacher_hidden, teacher_down, teacher_gain, student_stream, contexts, proj_weight, student_gain, head_weight):
    teacher_sum = jnp.dot(teacher_hidden, teacher_down, preferred_element_type=jnp.float32)
    target = normalize(teacher_sum, teacher_gain)[0].astype(jnp.bfloat16)
    stream = student_stream.astype(jnp.float32) + jnp.einsum('lrc,lcd->rd', contexts.astype(jnp.float32), proj_weight.astype(jnp.float32))
    scaled, normed, inv_std = normalize(stream, student_gain)
    features = scaled.astype(jnp.bfloat16)
    predicted = jnp.dot(features, head_weight, preferred_element_type=jnp.float32)
    pred_grad = ((predicted - target.astype(jnp.float32)) * (1.0 / math.sqrt(TOKENS))).astype(jnp.bfloat16)
    head_grad = jnp.dot(features.T, pred_grad, preferred_element_type=jnp.float32)
    feature_grad = jnp.dot(pred_grad, head_weight.T, preferred_element_type=jnp.float32)
    stream_grad = normalize_back(feature_grad, student_gain, normed, inv_std).astype(jnp.bfloat16)
    proj_grad = jnp.einsum('lrc,rd->lcd', contexts.astype(jnp.float32), stream_grad.astype(jnp.float32))
    return (head_grad, proj_grad)
```

```python
import functools
import math

import jax
import jax.numpy as jnp
from jax import lax
from jax.experimental import pallas as pl
from jax.experimental.pallas import tpu as pltpu
from jax.sharding import PartitionSpec as P

MESH = pl.DeviceIdType.MESH
F32 = jnp.float32
BF16 = jnp.bfloat16
EPS = 1e-06
OWN, PAD = 40, 48
SCALE = 1.0 / math.sqrt(5120)


def dot(a, b):
    return jnp.dot(a, b, preferred_element_type=F32)


def dot_nt(a, b):
    return lax.dot_general(a, b, (((1,), (1,)), ((), ())), preferred_element_type=F32)


def dot_tn(a, b):
    return lax.dot_general(a, b, (((0,), (0,)), ((), ())), preferred_element_type=F32)


def kernel(
    hid, down, tgain, stream_in, ctx, pw, sgain, headt,
    hg_out, pg_out,
    hid_v, down_v,
    send1, own1, rly1, land1,
    send2, own2, rly2, land2,
    send3, land3,
    tsum,
    ctx_s, ctx_r, ctx_f,
    wk, hk,
    st_s, st_r, feat_s, feat_r, fwide,
    normed_v, istd_v, pred,
    tpad, stat, rpad, grad,
    fg, fg_s, fg_r, sg_s, sg_r, sgw,
    hx, hcr, hy, hyo, hzr, hz, hxr,
    px, pcr, py, pyo, pzr, pz, pxr,
    hfin, pfin,
    lsem, ssem, rsem,
):
    dp = lax.axis_index("dp")
    t = lax.axis_index("tensor")
    h, c = dp // 2, dp % 2
    xl, y, z = t // 16, (t // 4) % 4, t % 4
    xx = 2 * h + xl

    def dev(h_, c_, xl_, y_, z_):
        return {"dp": h_ * 2 + c_, "tensor": xl_ * 16 + y_ * 4 + z_}

    def dev_y(k):
        return dev(h, c, xl, (y + k) % 4, z)

    def dev_z(k):
        return dev(h, c, xl, y, (z + k) % 4)

    def dev_x(k):
        n = (xx + k) % 4
        return dev(n // 2, c, n % 2, y, z)

    xlo = dev(h, c, 1 - xl, y, z)
    other = dev(h, 1 - c, xl, y, z)

    slots = [0]
    copies = []

    def send(src, dst, to):
        i = slots[0]
        slots[0] += 1
        copy = pltpu.make_async_remote_copy(
            src_ref=src, dst_ref=dst, send_sem=ssem.at[i], recv_sem=rsem.at[i],
            device_id=to, device_id_type=MESH,
        )
        copy.start()
        copies.append(copy)
        return copy

    loads = []

    def load(src, dst):
        copy = pltpu.make_async_copy(src, dst, lsem.at[len(loads)])
        copy.start()
        loads.append(copy)

    load(hid, hid_v)

    def dcol(half, q):
        return down.at[:, pl.ds(pl.multiple_of(1536 * half + 384 * q, 128), 384)]

    load(dcol(0, (y + 2) % 4), down_v.at[0, 2])
    for q in range(4):
        load(dcol(1, q), down_v.at[1, q])
    for k in (1, 3, 0):
        load(dcol(0, (y + k) % 4), down_v.at[0, k])

    barrier = pltpu.get_barrier_semaphore()
    for to in (
        [dev_y(k) for k in (1, 2, 3)] + [dev_z(k) for k in (1, 2, 3)]
        + [dev_x(k) for k in (1, 2, 3)] + [other]
    ):
        pl.semaphore_signal(barrier, 1, device_id=to, device_id_type=MESH)

    fill = jnp.zeros((16, 1024), BF16)
    for buf in (st_s, fg_s):
        for k in range(buf.shape[0]):
            buf[k, 32:48, :] = fill
    feat_s[32:48, :] = fill
    sg_s[32:48, :] = fill
    for k in range(4):
        for j in range(4):
            ctx_s[k, j, 32:48, :] = fill[:, :128]
    tpad[...] = jnp.zeros_like(tpad)
    rpad[...] = jnp.zeros_like(rpad)

    for k in range(4):
        q = (y + k) % 4
        for layer in range(2):
            for half in range(2):
                cols = pl.ds(pl.multiple_of(512 * half + 128 * q, 128), 128)
                ctx_s[k, 2 * layer + half, 0:OWN, :] = ctx[layer, :, cols]
    pl.semaphore_wait(barrier, 10)

    ctx_c = [send(ctx_s.at[k], ctx_r.at[y], dev_y(k)) for k in (2, 1, 3)]
    ctx_r[y] = ctx_s[0]

    lanes = pl.ds(pl.multiple_of(512 * c, 128), 512)
    wz_c = [send(pw.at[:, :, lanes], wk.at[:, xl, z, :, lanes], dev_z(k)) for k in (2, 1, 3)]
    hz_c = [send(headt.at[:, lanes], hk.at[xl, z, :, lanes], dev_z(k)) for k in (2, 1, 3)]
    wk[:, xl, z, :, lanes] = pw[:, :, lanes]
    hk[xl, z, :, lanes] = headt[:, lanes]

    def product(ab, k):
        def tile(i, carry):
            if ab == 0:
                value = dot(hid_v[i], down_v[0, k])
            else:
                value = dot(hid_v[(z + k) % 4], down_v[1, i])
            if k == 0:
                own1[ab, i] = value
            else:
                send1[ab, k - 1, i] = value.astype(BF16)
            return carry

        lax.fori_loop(0, 4, tile, 0)

    def ring(ab, n):
        return dev_y if (ab == 0) == (n == 4) else dev_z

    def relay_out(sbuf, rly, ab, n):
        to = ring(ab, n)
        m = n // 2
        return [
            send(sbuf.at[ab, 1, pl.ds(0, m)], rly.at[ab, 0], to(1)),
            send(sbuf.at[ab, 1, pl.ds(m, m)], rly.at[ab, 1], to(3)),
        ]

    def direct_out(sbuf, land, ab, n, k):
        to = ring(ab, n)
        m = n // 2
        if k == 1:
            return send(sbuf.at[ab, 0, pl.ds(m, m)], land.at[ab, 0, pl.ds(m, m)], to(1))
        return send(sbuf.at[ab, 2, pl.ds(0, m)], land.at[ab, 1, pl.ds(0, m)], to(3))

    def relay_on(sbuf, rly, land, ab, n, arrivals):
        to = ring(ab, n)
        m = n // 2
        out = []
        arrivals[0].wait_recv()
        for i in range(m):
            sbuf[ab, 0, i] = (sbuf[ab, 0, i].astype(F32) + rly[ab, 0, i].astype(F32)).astype(BF16)
        out.append(send(sbuf.at[ab, 0, pl.ds(0, m)], land.at[ab, 0, pl.ds(0, m)], to(1)))
        arrivals[1].wait_recv()
        for i in range(m):
            sbuf[ab, 2, m + i] = (sbuf[ab, 2, m + i].astype(F32) + rly[ab, 1, i].astype(F32)).astype(BF16)
        out.append(send(sbuf.at[ab, 2, pl.ds(m, m)], land.at[ab, 1, pl.ds(m, m)], to(3)))
        return out

    loads[0].wait()
    loads[1].wait()
    product(0, 2)
    r1 = [relay_out(send1, rly1, 0, 4), None]
    for i in range(2, 6):
        loads[i].wait()
    product(1, 2)
    r1[1] = relay_out(send1, rly1, 1, 4)
    d1 = [[], []]
    for i in range(6, 9):
        loads[i].wait()
    product(0, 1)
    d1[0].append(direct_out(send1, land1, 0, 4, 1))
    product(0, 3)
    d1[0].append(direct_out(send1, land1, 0, 4, 3))
    product(1, 1)
    d1[1].append(direct_out(send1, land1, 1, 4, 1))
    product(1, 3)
    d1[1].append(direct_out(send1, land1, 1, 4, 3))

    for w in ctx_c:
        w.wait_recv()
    for q in range(4):
        for j in range(4):
            ctx_f[OWN * q : OWN * q + OWN, 128 * j : 128 * j + 128] = ctx_r[q, j].astype(F32)[0:OWN]
    d1[0] += relay_on(send1, rly1, land1, 0, 4, r1[0])
    d1[1] += relay_on(send1, rly1, land1, 1, 4, r1[1])
    for w in wz_c + hz_c:
        w.wait_recv()
    wx_c = [
        send(wk.at[:, xl, :, :, lanes], wk.at[:, xl, :, :, lanes], xlo),
        send(hk.at[xl, :, :, lanes], hk.at[xl, :, :, lanes], xlo),
    ]
    product(0, 0)
    product(1, 0)
    wx_c[0].wait_recv()
    wc_c = [send(wk.at[:, :, :, :, lanes], wk.at[:, :, :, :, lanes], other)]
    wx_c[1].wait_recv()
    wc_c.append(send(hk.at[:, :, :, lanes], hk.at[:, :, :, lanes], other))
    wc_c[0].wait_recv()
    part = dot(ctx_f[...].astype(BF16), wk[...].reshape(512, 1024))
    fg[...] = part.reshape(4, OWN, 1024)
    for k in (2, 1, 3):
        st_s[k - 1, 0:OWN, :] = fg[(y + k) % 4].astype(BF16)
    st_c = [send(st_s.at[k - 1], st_r.at[k - 1], dev_y(k)) for k in (2, 1, 3)]
    stream = stream_in[...].astype(F32) + fg[y]
    for w in st_c:
        w.wait_recv()
    for k in range(3):
        stream = stream + st_r[k].astype(F32)[0:OWN]
    centered = stream - jnp.mean(stream, axis=-1, keepdims=True)
    istd = lax.rsqrt(jnp.mean(centered * centered, axis=-1, keepdims=True) + EPS)
    normed = centered * istd
    normed_v[...] = normed
    istd_v[...] = jnp.broadcast_to(istd, istd_v.shape)
    feat_s[0:OWN, :] = (normed * sgain[...]).astype(BF16)
    ft_c = [send(feat_s, feat_r.at[y], dev_y(k)) for k in (2, 1, 3)]
    feat_r[y] = feat_s[...]

    for ab in range(2):
        for w in d1[ab]:
            w.wait_recv()

    def total1(ab, k):
        q = ((z if ab == 0 else y) + k) % 4
        value = own1[ab, q] + land1[ab, 0, q].astype(F32) + land1[ab, 1, q].astype(F32)
        if k == 0:
            own2[ab] = value.reshape(2, 160, 384)
        else:
            send2[ab, k - 1] = value.reshape(2, 160, 384).astype(BF16)

    r2, d2 = [None, None], [[], []]
    for ab in range(2):
        total1(ab, 2)
        r2[ab] = relay_out(send2, rly2, ab, 2)
    for ab in range(2):
        for k in (1, 3):
            total1(ab, k)
            d2[ab].append(direct_out(send2, land2, ab, 2, k))
    for ab in range(2):
        total1(ab, 0)
    for ab in range(2):
        d2[ab] += relay_on(send2, rly2, land2, ab, 2, r2[ab])

    for w in ft_c:
        w.wait_recv()
    for q in range(4):
        fwide[OWN * q : OWN * q + OWN, :] = feat_r[q].astype(F32)[0:OWN]
    feats = fwide[...].astype(BF16)
    wc_c[1].wait_recv()
    pred[...] = dot_nt(feats, hk[...].reshape(768, 1024))

    for ab in range(2):
        for w in d2[ab]:
            w.wait_recv()

    def total2(ab, q):
        return own2[ab, q] + land2[ab, 0, q].astype(F32) + land2[ab, 1, q].astype(F32)

    x3 = []
    for ab in range(2):
        send3[ab] = total2(ab, 1 - xl).astype(BF16)
        x3.append(send(send3.at[ab], land3.at[ab], xlo))
    for ab in range(2):
        tsum[:, 384 * ab : 384 * ab + 384] = total2(ab, xl)
    for ab in range(2):
        x3[ab].wait_recv()
        tsum[:, 384 * ab : 384 * ab + 384] += land3[ab].astype(F32)

    teach = tsum[...]
    mean_own = jnp.mean(teach, axis=-1, keepdims=True)
    cent = teach - mean_own
    m2_own = jnp.sum(cent * cent, axis=-1, keepdims=True)
    lane = lax.broadcasted_iota(jnp.int32, (160, 128), 1)
    tpad[0:160, :] = jnp.where(lane == 0, mean_own, jnp.where(lane == 1, m2_own, 0.0))
    stat[0] = tpad[...].T[0:8, :]
    sc = [send(stat.at[0], stat.at[k], dev_y(k)) for k in (2, 1, 3)]
    for w in sc:
        w.wait_recv()
    means = [stat[k, 0:1, :] for k in range(4)]
    mean_row = (means[0] + means[1] + means[2] + means[3]) * 0.25
    m2_row = sum(stat[k, 1:2, :] for k in range(4)) + 768.0 * sum((m - mean_row) ** 2 for m in means)
    rpad[0:1, :] = mean_row
    rpad[1:2, :] = lax.rsqrt(m2_row * (1.0 / 3072) + EPS)
    cols = rpad[...].T
    mean_col, istd_col = cols[0:160, 0:1], cols[0:160, 1:2]
    for half in range(2):
        s = slice(384 * half, 384 * half + 384)
        target = ((tsum[:, s] - mean_col) * istd_col * tgain[half, y]).astype(BF16)
        grad[:, s] = ((pred[:, s] - target.astype(F32)) * SCALE).astype(BF16)

    grads = grad[...]
    fg[...] = dot(grads, hk[...].reshape(768, 1024)).reshape(4, OWN, 1024)
    for k in (2, 1, 3):
        fg_s[k - 1, 0:OWN, :] = fg[(y + k) % 4].astype(BF16)
    fg_c = [send(fg_s.at[k - 1], fg_r.at[k - 1], dev_y(k)) for k in (2, 1, 3)]

    hgt = dot_tn(grads, feats).astype(BF16)
    for half in range(2):
        hx[half] = hgt[:, 512 * half : 512 * half + 512].reshape(2, 4, 96, 512)

    def core_out(xbuf, crbuf):
        return send(xbuf.at[1 - c], crbuf, other)

    def z_out(xbuf, crbuf, ybuf, yown, zrbuf, arrival):
        arrival.wait_recv()
        out = []
        for k in (2, 1, 3, 0):
            q = (z + k) % 4
            value = xbuf[c, :, q].astype(F32) + crbuf[:, q].astype(F32)
            if k == 0:
                yown[...] = value
            else:
                ybuf[k - 1] = value.astype(BF16)
                out.append(send(ybuf.at[k - 1], zrbuf.at[k - 1], dev_z(k)))
        return out

    def x_out(yown, zrbuf, zbuf, xrbuf, arrivals):
        for w in arrivals:
            w.wait_recv()
        value = yown[...] + zrbuf[0].astype(F32) + zrbuf[1].astype(F32) + zrbuf[2].astype(F32)
        zbuf[...] = value.astype(BF16)
        out = [
            send(zbuf.at[1 - xl if k % 2 else xl], xrbuf.at[xx], dev_x(k)) for k in (2, 1, 3)
        ]
        xrbuf[xx] = zbuf[xl]
        return out

    def last(xrbuf, fin, arrivals):
        for w in arrivals:
            w.wait_recv()
        fin[c] = (xrbuf[0].astype(F32) + xrbuf[1].astype(F32)) + (xrbuf[2].astype(F32) + xrbuf[3].astype(F32))
        return send(fin.at[c], fin.at[c], other)

    hc_c = core_out(hx, hcr)

    gsum = fg[y]
    for w in fg_c:
        w.wait_recv()
    for k in range(3):
        gsum = gsum + fg_r[k].astype(F32)[0:OWN]
    weighted = gsum * sgain[...]
    nrm = normed_v[...]
    first = jnp.mean(weighted, axis=-1, keepdims=True)
    second = jnp.mean(weighted * nrm, axis=-1, keepdims=True)
    sg_s[0:OWN, :] = (istd_v[:, 0:1] * (weighted - first - nrm * second)).astype(BF16)
    sg_c = [send(sg_s, sg_r.at[y], dev_y(k)) for k in (2, 1, 3)]
    sg_r[y] = sg_s[...]

    hzc = z_out(hx, hcr, hy, hyo, hzr, hc_c)

    for w in sg_c:
        w.wait_recv()
    for q in range(4):
        sgw[OWN * q : OWN * q + OWN, :] = sg_r[q].astype(F32)[0:OWN]
    sgrads = sgw[...].astype(BF16)
    for layer in range(2):
        for half in range(2):
            j = 2 * layer + half
            block = ctx_f[:, 128 * j : 128 * j + 128].astype(BF16)
            value = dot_tn(block, sgrads).astype(BF16)
            for s in range(2):
                px[s, half, :, layer] = value[:, 512 * s : 512 * s + 512].reshape(4, 32, 512)
    pc_c = core_out(px, pcr)
    hxc = x_out(hyo, hzr, hz, hxr, hzc)
    pzc = z_out(px, pcr, py, pyo, pzr, pc_c)
    hlast = last(hxr, hfin, hxc)
    pxc = x_out(pyo, pzr, pz, pxr, pzc)
    plast = last(pxr, pfin, pxc)
    hlast.wait_recv()
    for s in range(2):
        hg_out[:, 512 * s : 512 * s + 512] = hfin[s]
    plast.wait_recv()
    for s in range(2):
        pg_out[:, :, 512 * s : 512 * s + 512] = pfin[s]
    for copy in copies:
        copy.wait_send()
    assert slots[0] <= N_SLOTS


N_SLOTS = 96


def per_device(
    teacher_hidden, teacher_down, teacher_gain, student_stream, contexts, proj_weight, student_gain, head_weight
):
    hid = teacher_hidden.reshape(2, 4, 4, OWN, 768).transpose(2, 0, 1, 3, 4).reshape(4, 320, 768)
    vmem = pl.BlockSpec(memory_space=pltpu.VMEM)
    hbm = pl.BlockSpec(memory_space=pl.ANY)

    def v(*shape, dtype=BF16):
        return pltpu.VMEM(shape, dtype)

    def reduce_bufs(n, tail):
        return [
            v(2, 2, 4, *tail), v(2, 4, *tail), v(3, 2, *tail), v(2, *tail, dtype=F32),
            v(3, 2, *tail), v(2, *tail), v(4, *tail),
        ]

    scratch = [
        v(4, 320, 768), v(2, 4, 768, 384),
        v(2, 3, 4, 320, 384), v(2, 4, 320, 384, dtype=F32), v(2, 2, 2, 320, 384), v(2, 2, 4, 320, 384),
        v(2, 3, 2, 160, 384), v(2, 2, 160, 384, dtype=F32), v(2, 2, 1, 160, 384), v(2, 2, 2, 160, 384),
        v(2, 160, 384), v(2, 160, 384),
        v(160, 768, dtype=F32),
        v(4, 4, PAD, 128), v(4, 4, PAD, 128), v(160, 512, dtype=F32),
        v(2, 2, 4, 32, 1024), v(2, 4, 96, 1024),
        v(3, PAD, 1024), v(3, PAD, 1024), v(PAD, 1024), v(4, PAD, 1024), v(160, 1024, dtype=F32),
        v(OWN, 1024, dtype=F32), v(OWN, 128, dtype=F32), v(160, 768, dtype=F32),
        v(256, 128, dtype=F32), v(4, 8, 256, dtype=F32), v(128, 256, dtype=F32), v(160, 768),
        v(4, OWN, 1024, dtype=F32), v(3, PAD, 1024), v(3, PAD, 1024), v(PAD, 1024), v(4, PAD, 1024),
        v(160, 1024, dtype=F32),
        *reduce_bufs(96, (96, 512)),
        *reduce_bufs(64, (2, 32, 512)),
        v(2, 96, 512, dtype=F32), v(2, 2, 32, 512, dtype=F32),
        pltpu.SemaphoreType.DMA((16,)), pltpu.SemaphoreType.DMA((N_SLOTS,)), pltpu.SemaphoreType.DMA((N_SLOTS,)),
    ]
    head_grad, proj_grad = pl.pallas_call(
        kernel,
        out_shape=(
            jax.ShapeDtypeStruct((96, 1024), F32),
            jax.ShapeDtypeStruct((2, 32, 1024), F32),
        ),
        in_specs=[hbm, hbm, vmem, vmem, vmem, vmem, vmem, vmem],
        out_specs=(vmem, vmem),
        scratch_shapes=scratch,
        compiler_params=pltpu.CompilerParams(
            collective_id=0, has_side_effects=True, vmem_limit_bytes=56 * 2**20
        ),
        cost_estimate=pl.CostEstimate(flops=6 * 10**9, bytes_accessed=8 * 10**6, transcendentals=0),
    )(
        hid,
        teacher_down,
        teacher_gain.reshape(2, 4, 1, 384),
        student_stream,
        contexts,
        proj_weight,
        student_gain.reshape(1, 1024),
        head_weight.T,
    )
    return head_grad.T, proj_grad


def solution(mesh):
    in_specs = (
        P("dp", "tensor"),
        P("tensor", None),
        P(),
        P(("dp", "tensor"), None),
        P(None, ("dp", "tensor"), None),
        P(None, "tensor", None),
        P(),
        P(None, "tensor"),
    )
    out_specs = (P(None, "tensor"), P(None, "tensor", None))
    return jax.shard_map(
        per_device, mesh=mesh, in_specs=in_specs, out_specs=out_specs, check_vma=False
    )
```

```python
import functools
import math

import jax
import jax.numpy as jnp
from jax import lax
from jax.experimental import pallas as pl
from jax.experimental.pallas import tpu as pltpu
from jax.sharding import PartitionSpec as P

MESH = pl.DeviceIdType.MESH
F32 = jnp.float32
BF16 = jnp.bfloat16
EPS = 1e-06
OWN = 40
SIDE = 64
MAIN = 160 - SIDE
SCALE = 1.0 / math.sqrt(5120)


def dot(a, b):
    return jnp.dot(a, b, preferred_element_type=F32)


def dot_nt(a, b):
    return lax.dot_general(a, b, (((1,), (1,)), ((), ())), preferred_element_type=F32)


def pack(v):
    return jnp.concatenate([v[:, 0:512], v[:, 512:1024]], axis=0).astype(BF16)


def unpack(b):
    v = b.astype(F32)
    return jnp.concatenate([v[0:OWN], v[OWN : 2 * OWN]], axis=1)


def dot_tn(a, b):
    return lax.dot_general(a, b, (((0,), (0,)), ((), ())), preferred_element_type=F32)


def kernel(
    hid, down, tgain, stream_in, ctx, pw, sgain, headt,
    hg_out, pg_out,
    hm_v, hs_v, down_v, down_b,
    msend1, mown1, mrly1, mland1, msend2, mown2, mland2,
    ssend1, sown1, srly1, sland1, ssend2, sown2, sland2,
    xs, xr, xown,
    send3, land3,
    tsum,
    strm_s, strm_r, ctx_s, ctx_r, ctx_f,
    wk, hk,
    st_s, st_r, feat_s, feat_r, fwide,
    normed_v, istd_v, pred,
    tpad, stat, rpad, grad,
    fg, fg_s, fg_r, sg_s, sg_r, sgw,
    hx, hcr, hy, hyo, hzr, hz, hxr,
    px0, pcr0, py0, pyo0, pzr0, pz0, pxr0,
    px1, pcr1, py1, pyo1, pzr1, pz1, pxr1,
    hfin, pfin,
    lsem, ssem, rsem, tsem, usem,
):
    dp = lax.axis_index("dp")
    t = lax.axis_index("tensor")
    h, c = dp // 2, dp % 2
    xl, y, z = t // 16, (t // 4) % 4, t % 4
    xx = 2 * h + xl

    def dev(h_, c_, xl_, y_, z_):
        return {"dp": h_ * 2 + c_, "tensor": xl_ * 16 + y_ * 4 + z_}

    def dev_y(k):
        return dev(h, c, xl, (y + k) % 4, z)

    def dev_z(k):
        return dev(h, c, xl, y, (z + k) % 4)

    def dev_x(k):
        n = (xx + k) % 4
        return dev(n // 2, c, n % 2, y, z)

    xlo = dev(h, c, 1 - xl, y, z)
    xhi = dev(1 - h, c, 1 - xl, y, z)
    other = dev(h, 1 - c, xl, y, z)

    slots = [0]
    copies = []

    def send(src, dst, to):
        i = slots[0]
        slots[0] += 1
        copy = pltpu.make_async_remote_copy(
            src_ref=src, dst_ref=dst, send_sem=ssem.at[i], recv_sem=rsem.at[i],
            device_id=to, device_id_type=MESH,
        )
        copy.start()
        copies.append(copy)
        return copy

    loads = []

    def load(src, dst):
        copy = pltpu.make_async_copy(src, dst, lsem.at[len(loads)])
        copy.start()
        loads.append(copy)

    def dcol(q):
        return down.at[:, pl.ds(pl.multiple_of(384 * q, 128), 384)]

    lanes = pl.ds(pl.multiple_of(512 * c, 128), 512)
    for half in range(2):
        load(hid.at[pl.ds(4 * half, 4), pl.ds(0, MAIN)], hm_v.at[:, half])
    load(dcol((y + 2) % 4), down_v.at[2])
    load(down.at[:, pl.ds(1536, 1536)], down_b)
    for half in range(2):
        load(hid.at[pl.ds(4 * half, 4), pl.ds(MAIN, SIDE)], hs_v.at[half])
    load(pw.at[:, :, lanes], wk.at[:, xl, z, :, lanes])
    load(headt.at[:, lanes], hk.at[xl, z, :, lanes])
    for k in (1, 3, 0):
        load(dcol((y + k) % 4), down_v.at[k])

    barrier = pltpu.get_barrier_semaphore()
    for to in (
        [dev_y(k) for k in (1, 2, 3)] + [dev_z(k) for k in (1, 2, 3)]
        + [dev_x(k) for k in (1, 2, 3)] + [other]
    ):
        pl.semaphore_signal(barrier, 1, device_id=to, device_id_type=MESH)
    for j in range(4):
        mine = jnp.where(jnp.logical_and(y == z, z == j), 1, 0)
        to = dev(h, c + mine * (1 - 2 * c), xl, z, j)
        pl.semaphore_signal(barrier, 1, device_id=to, device_id_type=MESH)

    tpad[...] = jnp.zeros_like(tpad)
    rpad[...] = jnp.zeros_like(rpad)

    def main_product(ab, k):
        if ab == 0:
            value = dot(hm_v[...].reshape(8 * MAIN, 768), down_v[k]).reshape(4, 2 * MAIN, 384)
            if k == 0:
                mown1[0] = value
            else:
                msend1[0, k - 1] = value.astype(BF16)
            return

        value = dot(hm_v[(z + k) % 4].reshape(2 * MAIN, 768), down_b[...])
        for i in range(4):
            block = value[:, 384 * i : 384 * i + 384]
            if k == 0:
                mown1[1, i] = block
            else:
                msend1[1, k - 1, i] = block.astype(BF16)

    def side_product_y(k, rows, out):
        out[0, k] = dot(hs_v[rows].reshape(4 * SIDE, 768), down_v[k]).reshape(4, SIDE, 384).astype(out.dtype)

    def side_product_z(rows, out):
        value = dot(hs_v[rows].reshape(4 * SIDE, 768), down_b[...]).reshape(4, SIDE, 1536).astype(out.dtype)
        for q in range(4):
            for i in range(4):
                out[1, (q - z + 4) % 4, i] = value[q, :, 384 * i : 384 * i + 384]

    class Ring:
        def __init__(self, to, ab, n, sbuf, rly, land):
            self.to, self.ab, self.n, self.m = to, ab, n, n // 2
            self.sbuf, self.rly, self.land = sbuf, rly, land
            self.relays, self.final = [], []

        def halves(self):
            return pl.ds(0, self.m), pl.ds(self.m, self.n - self.m)

        def relay_out(self):
            low, high = self.halves()
            for d, part in ((0, low), (1, high)):
                self.relays.append(
                    send(self.sbuf.at[self.ab, 1, part], self.rly.at[self.ab, d, part], self.to(1 + 2 * d))
                )

        def direct_out(self, k):
            low, high = self.halves()
            d, part = (0, high) if k == 1 else (1, low)
            self.final.append(
                send(self.sbuf.at[self.ab, k - 1, part], self.land.at[self.ab, d, part], self.to(k))
            )

        def relay_on(self):
            low, high = self.halves()
            for d, k, part, slabs in (
                (0, 1, low, range(self.m)),
                (1, 3, high, range(self.m, self.n)),
            ):
                self.relays[d].wait_recv()
                for i in slabs:
                    value = self.sbuf[self.ab, k - 1, i].astype(F32) + self.rly[self.ab, d, i].astype(F32)
                    self.sbuf[self.ab, k - 1, i] = value.astype(BF16)
                self.final.append(
                    send(self.sbuf.at[self.ab, k - 1, part], self.land.at[self.ab, d, part], self.to(k))
                )

        def finish(self):
            for w in self.final:
                w.wait_recv()

    main1 = [Ring(dev_y, 0, 4, msend1, mrly1, mland1), Ring(dev_z, 1, 4, msend1, mrly1, mland1)]
    side1 = [Ring(dev_y, 0, 4, ssend1, srly1, sland1), Ring(dev_z, 1, 4, ssend1, srly1, sland1)]

    for i in range(3):
        loads[i].wait()
    main_product(0, 2)
    pl.semaphore_wait(barrier, 14)
    main1[0].relay_out()
    for i in range(3, 6):
        loads[i].wait()
    main_product(1, 2)
    main1[1].relay_out()
    xc = [[None] * 4, [None] * 4]

    def x_first(ab, k):
        xc[ab][k] = send(xs.at[ab, k], xr.at[ab, k], xlo)

    side_product_y(2, 1 - xl, xs)
    x_first(0, 2)

    strm_s[...] = pack(stream_in[...].astype(F32))
    for q in range(4):
        parts = [
            ctx[layer, :, 512 * half + 128 * q : 512 * half + 128 * q + 128].astype(F32)
            for layer in range(2)
            for half in range(2)
        ]
        ctx_s[q] = jnp.concatenate(parts, axis=0).astype(BF16)
    strm_self = jnp.logical_and(y == z, z == y)
    strm_to = pltpu.make_async_remote_copy(
        src_ref=strm_s, dst_ref=strm_r, send_sem=usem.at[8], recv_sem=usem.at[9],
        device_id=dev(h, c, xl, z, y), device_id_type=MESH,
    )

    @pl.when(strm_self)
    def _():
        pltpu.make_async_copy(strm_s, strm_r, usem.at[9]).start()

    @pl.when(jnp.logical_not(strm_self))
    def _():
        strm_to.start()

    ctx_to = []
    for q in range(4):
        mine = jnp.logical_and(y == z, y == q)
        copy = pltpu.make_async_remote_copy(
            src_ref=ctx_s.at[q], dst_ref=ctx_r.at[z], send_sem=usem.at[q], recv_sem=tsem.at[z],
            device_id=dev(h, c, xl, q, y), device_id_type=MESH,
        )
        ctx_to.append((mine, copy))

        @pl.when(mine)
        def _():
            pltpu.make_async_copy(ctx_s.at[q], ctx_r.at[z], tsem.at[z]).start()

        @pl.when(jnp.logical_not(mine))
        def _():
            copy.start()

    loads[6].wait()
    wz_c = [send(wk.at[:, xl, z, :, lanes], wk.at[:, xl, z, :, lanes], dev_z(k)) for k in (2, 1, 3)]
    side_product_z(1 - xl, xs)
    x_first(1, 2)
    for i in range(7, 11):
        loads[i].wait()
    for ab in range(2):
        for k in (1, 3):
            main_product(ab, k)
            main1[ab].direct_out(k)
    for k in (1, 3, 0):
        side_product_y(k, 1 - xl, xs)
        x_first(0, k)
        x_first(1, k)
    main_product(0, 0)
    main_product(1, 0)
    for k in (2, 1, 3, 0):
        side_product_y(k, xl, xown)
    side_product_z(xl, xown)
    for ab in range(2):
        main1[ab].relay_on()
    hz_c = [send(hk.at[xl, z, :, lanes], hk.at[xl, z, :, lanes], dev_z(k)) for k in (2, 1, 3)]

    def side_add(ab, k):
        xc[ab][k].wait_recv()
        value = xown[ab, k] + xr[ab, k].astype(F32)
        if k == 0:
            sown1[ab] = value
        else:
            ssend1[ab, k - 1] = value.astype(BF16)

    for ab in range(2):
        side_add(ab, 2)
        side1[ab].relay_out()
    for w in wz_c:
        w.wait_recv()
    wx_c = [send(wk.at[:, xl, :, :, lanes], wk.at[:, xl, :, :, lanes], xhi)]
    for ab in range(2):
        side_add(ab, 1)
        side1[ab].direct_out(1)

    for j in range(4):
        pltpu.make_async_remote_copy(
            src_ref=ctx_s.at[j], dst_ref=ctx_r.at[j], send_sem=usem.at[j], recv_sem=tsem.at[j],
            device_id=dev(h, c, xl, j, y), device_id_type=MESH,
        ).wait_recv()
        block = ctx_r[j].astype(F32)
        for i in range(4):
            ctx_f[OWN * j : OWN * j + OWN, 128 * i : 128 * i + 128] = block[OWN * i : OWN * i + OWN]
    wx_c[0].wait_recv()
    wc_c = [send(wk.at[:, :, :, :, lanes], wk.at[:, :, :, :, lanes], other)]
    wc_c[0].wait_recv()
    fg[...] = dot(ctx_f[...].astype(BF16), wk[...].reshape(512, 1024)).reshape(4, OWN, 1024)
    for k in (2, 1, 3):
        st_s[k - 1] = pack(fg[(y + k) % 4])
    st_c = [send(st_s.at[k - 1], st_r.at[k - 1], dev_y(k)) for k in (2, 1, 3)]

    def second(part, first, ab):
        own1, land1, own2, send2, land2 = part
        first[ab].finish()
        out = []
        for k in (2, 1, 3, 0):
            q = ((z if ab == 0 else y) + k) % 4
            value = own1[ab, q] + land1[ab, 0, q].astype(F32) + land1[ab, 1, q].astype(F32)
            value = value.reshape(own2.shape[1:])
            if k == 0:
                own2[ab] = value
            else:
                send2[ab, k - 1] = value.astype(BF16)
                to = dev_z(k) if ab == 0 else dev_y(k)
                out.append(send(send2.at[ab, k - 1], land2.at[ab, k - 1], to))
        return out

    main_part = (mown1, mland1, mown2, msend2, mland2)
    side_part = (sown1, sland1, sown2, ssend2, sland2)
    main2, side2 = [None, None], [None, None]
    side_add(0, 3)
    side1[0].direct_out(3)
    side1[0].relay_on()
    main2[0] = second(main_part, main1, 0)
    side_add(1, 3)
    side1[1].direct_out(3)
    side1[1].relay_on()
    main2[1] = second(main_part, main1, 1)
    for w in hz_c:
        w.wait_recv()
    wx_c.append(send(hk.at[xl, :, :, lanes], hk.at[xl, :, :, lanes], xhi))
    strm_to.wait_recv()
    stream = unpack(strm_r[...]) + fg[y]
    for w in st_c:
        w.wait_recv()
    for k in range(3):
        stream = stream + unpack(st_r[k])
    centered = stream - jnp.mean(stream, axis=-1, keepdims=True)
    istd = lax.rsqrt(jnp.mean(centered * centered, axis=-1, keepdims=True) + EPS)
    normed = centered * istd
    normed_v[...] = normed
    istd_v[...] = jnp.broadcast_to(istd, istd_v.shape)
    feat_s[...] = pack(normed * sgain[...])
    ft_c = [send(feat_s, feat_r.at[y], dev_y(k)) for k in (2, 1, 3)]
    feat_r[y] = feat_s[...]
    for ab in range(2):
        side_add(ab, 0)
        side2[ab] = second(side_part, side1, ab)

    def total2(own2, land2, ab, q):
        value = own2[ab, q]
        for k in range(3):
            value = value + land2[ab, k, q].astype(F32)
        return value

    x3 = []
    for ab in range(2):
        for w in main2[ab]:
            w.wait_recv()
        send3[ab] = total2(mown2, mland2, ab, 1 - xl).astype(BF16)
        x3.append(send(send3.at[ab], land3.at[ab], xlo))
    wx_c[1].wait_recv()
    wc_c.append(send(hk.at[:, :, :, lanes], hk.at[:, :, :, lanes], other))

    for w in ft_c:
        w.wait_recv()
    for q in range(4):
        fwide[OWN * q : OWN * q + OWN, :] = unpack(feat_r[q])
    feats = fwide[...].astype(BF16)
    wc_c[1].wait_recv()
    pred[...] = dot_nt(feats, hk[...].reshape(768, 1024))
    for ab in range(2):
        s = slice(384 * ab, 384 * ab + 384)
        for w in side2[ab]:
            w.wait_recv()
        tsum[MAIN:160, s] = total2(sown2, sland2, ab, 0)
        x3[ab].wait_recv()
        tsum[0:MAIN, s] = total2(mown2, mland2, ab, xl) + land3[ab].astype(F32)

    teach = tsum[...]
    mean_own = jnp.mean(teach, axis=-1, keepdims=True)
    cent = teach - mean_own
    m2_own = jnp.sum(cent * cent, axis=-1, keepdims=True)
    lane = lax.broadcasted_iota(jnp.int32, (160, 128), 1)
    tpad[0:160, :] = jnp.where(lane == 0, mean_own, jnp.where(lane == 1, m2_own, 0.0))
    stat[0] = tpad[...].T[0:8, :]
    sc = [send(stat.at[0], stat.at[k], dev_y(k)) for k in (2, 1, 3)]
    for w in sc:
        w.wait_recv()
    means = [stat[k, 0:1, :] for k in range(4)]
    mean_row = (means[0] + means[1] + means[2] + means[3]) * 0.25
    m2_row = sum(stat[k, 1:2, :] for k in range(4)) + 768.0 * sum((m - mean_row) ** 2 for m in means)
    rpad[0:1, :] = mean_row
    rpad[1:2, :] = lax.rsqrt(m2_row * (1.0 / 3072) + EPS)
    cols = rpad[...].T
    mean_col, istd_col = cols[0:160, 0:1], cols[0:160, 1:2]
    for half in range(2):
        s = slice(384 * half, 384 * half + 384)
        target = ((tsum[:, s] - mean_col) * istd_col * tgain[half, y]).astype(BF16)
        grad[:, s] = ((pred[:, s] - target.astype(F32)) * SCALE).astype(BF16)

    grads = grad[...]
    fg[...] = dot(grads, hk[...].reshape(768, 1024)).reshape(4, OWN, 1024)
    for k in (2, 1, 3):
        fg_s[k - 1] = pack(fg[(y + k) % 4])
    fg_c = [send(fg_s.at[k - 1], fg_r.at[k - 1], dev_y(k)) for k in (2, 1, 3)]

    hgt = dot_tn(grads, feats).astype(BF16)
    for half in range(2):
        hx[half] = hgt[:, 512 * half : 512 * half + 512].reshape(2, 4, 96, 512)

    def core_out(xbuf, crbuf):
        return send(xbuf.at[1 - c], crbuf, other)

    def z_out(xbuf, crbuf, ybuf, yown, zrbuf, arrival):
        arrival.wait_recv()
        out = []
        for k in (2, 1, 3, 0):
            q = (z + k) % 4
            value = xbuf[c, :, q].astype(F32) + crbuf[:, q].astype(F32)
            if k == 0:
                yown[...] = value
            else:
                ybuf[k - 1] = value.astype(BF16)
                out.append(send(ybuf.at[k - 1], zrbuf.at[k - 1], dev_z(k)))
        return out

    def x_out(yown, zrbuf, zbuf, xrbuf, arrivals):
        for w in arrivals:
            w.wait_recv()
        value = yown[...] + zrbuf[0].astype(F32) + zrbuf[1].astype(F32) + zrbuf[2].astype(F32)
        zbuf[...] = value.astype(BF16)
        out = [
            send(zbuf.at[1 - xl if k % 2 else xl], xrbuf.at[xx], dev_x(k)) for k in (2, 1, 3)
        ]
        xrbuf[xx] = zbuf[xl]
        return out

    def last(xrbuf, fin, arrivals):
        for w in arrivals:
            w.wait_recv()
        fin[c] = (xrbuf[0].astype(F32) + xrbuf[1].astype(F32)) + (xrbuf[2].astype(F32) + xrbuf[3].astype(F32))
        return send(fin.at[c], fin.at[c], other)

    hc_c = core_out(hx, hcr)

    gsum = fg[y]
    for w in fg_c:
        w.wait_recv()
    for k in range(3):
        gsum = gsum + unpack(fg_r[k])
    weighted = gsum * sgain[...]
    nrm = normed_v[...]
    first = jnp.mean(weighted, axis=-1, keepdims=True)
    second = jnp.mean(weighted * nrm, axis=-1, keepdims=True)
    sg_s[...] = pack(istd_v[:, 0:1] * (weighted - first - nrm * second))
    sg_c = [send(sg_s, sg_r.at[y], dev_y(k)) for k in (2, 1, 3)]
    sg_r[y] = sg_s[...]

    hzc = z_out(hx, hcr, hy, hyo, hzr, hc_c)

    for w in sg_c:
        w.wait_recv()
    for q in range(4):
        sgw[OWN * q : OWN * q + OWN, :] = unpack(sg_r[q])
    sgrads = sgw[...].astype(BF16)
    pbufs = (
        (px0, pcr0, py0, pyo0, pzr0, pz0, pxr0),
        (px1, pcr1, py1, pyo1, pzr1, pz1, pxr1),
    )
    pc_c = []
    for layer in range(2):
        px = pbufs[layer][0]
        for half in range(2):
            j = 2 * layer + half
            block = ctx_f[:, 128 * j : 128 * j + 128].astype(BF16)
            value = dot_tn(block, sgrads).astype(BF16)
            for s in range(2):
                px[s, half] = value[:, 512 * s : 512 * s + 512].reshape(4, 32, 512)
        pc_c.append(core_out(px, pbufs[layer][1]))
    pzc = []
    for layer in range(2):
        px, pcr, py, pyo, pzr, pz, pxr = pbufs[layer]
        pzc.append(z_out(px, pcr, py, pyo, pzr, pc_c[layer]))
    hxc = x_out(hyo, hzr, hz, hxr, hzc)
    pxc = []
    for layer in range(2):
        px, pcr, py, pyo, pzr, pz, pxr = pbufs[layer]
        pxc.append(x_out(pyo, pzr, pz, pxr, pzc[layer]))
    hlast = last(hxr, hfin, hxc)
    plast = [last(pbufs[layer][6], pfin.at[layer], pxc[layer]) for layer in range(2)]
    hlast.wait_recv()
    for s in range(2):
        hg_out[:, 512 * s : 512 * s + 512] = hfin[s]
    for layer in range(2):
        plast[layer].wait_recv()
        for s in range(2):
            pg_out[layer, :, 512 * s : 512 * s + 512] = pfin[layer, s]
    for copy in copies:
        copy.wait_send()

    @pl.when(jnp.logical_not(strm_self))
    def _():
        strm_to.wait_send()

    for mine, copy in ctx_to:

        @pl.when(jnp.logical_not(mine))
        def _():
            copy.wait_send()

    assert slots[0] <= N_SLOTS


N_SLOTS = 128


def emit(hg_in, pg_in, hg_out, pg_out, sem):
    copies = [
        pltpu.make_async_copy(hg_in, hg_out, sem.at[0]),
        pltpu.make_async_copy(pg_in, pg_out, sem.at[1]),
    ]
    for copy in copies:
        copy.start()
    for copy in copies:
        copy.wait()


def per_device(
    teacher_hidden, teacher_down, teacher_gain, student_stream, contexts, proj_weight, student_gain, head_weight
):
    vmem = pl.BlockSpec(memory_space=pltpu.VMEM)
    hbm = pl.BlockSpec(memory_space=pl.ANY)

    def v(*shape, dtype=BF16):
        return pltpu.VMEM(shape, dtype)

    def reduce_bufs(tail):
        return [
            v(2, 2, 4, *tail), v(2, 4, *tail), v(3, 2, *tail), v(2, *tail, dtype=F32),
            v(3, 2, *tail), v(2, *tail), v(4, *tail),
        ]

    def ring_bufs(rows, n, r):
        return [
            v(2, 3, 4, rows, 384), v(2, 4, rows, 384, dtype=F32), v(2, 2, 4, rows, 384), v(2, 2, 4, rows, 384),
            v(2, 3, n, r, 384), v(2, n, r, 384, dtype=F32), v(2, 3, n, r, 384),
        ]

    scratch = [
        v(4, 2, MAIN, 768), v(2, 4, SIDE, 768), v(4, 768, 384), v(768, 1536),
        *ring_bufs(2 * MAIN, 2, MAIN),
        *ring_bufs(SIDE, 1, SIDE),
        v(2, 4, 4, SIDE, 384), v(2, 4, 4, SIDE, 384), v(2, 4, 4, SIDE, 384, dtype=F32),
        v(2, MAIN, 384), v(2, MAIN, 384),
        v(160, 768, dtype=F32),
        v(80, 512), v(80, 512), v(4, 160, 128), v(4, 160, 128), v(160, 512, dtype=F32),
        v(2, 2, 4, 32, 1024), v(2, 4, 96, 1024),
        v(3, 80, 512), v(3, 80, 512), v(80, 512), v(4, 80, 512), v(160, 1024, dtype=F32),
        v(OWN, 1024, dtype=F32), v(OWN, 128, dtype=F32), v(160, 768, dtype=F32),
        v(256, 128, dtype=F32), v(4, 8, 256, dtype=F32), v(128, 256, dtype=F32), v(160, 768),
        v(4, OWN, 1024, dtype=F32), v(3, 80, 512), v(3, 80, 512), v(80, 512), v(4, 80, 512),
        v(160, 1024, dtype=F32),
        *reduce_bufs((96, 512)),
        *reduce_bufs((32, 512)),
        *reduce_bufs((32, 512)),
        v(2, 96, 512, dtype=F32), v(2, 2, 32, 512, dtype=F32),
        pltpu.SemaphoreType.DMA((16,)), pltpu.SemaphoreType.DMA((N_SLOTS,)), pltpu.SemaphoreType.DMA((N_SLOTS,)),
        pltpu.SemaphoreType.DMA((4,)), pltpu.SemaphoreType.DMA((10,)),
    ]
    head_grad, proj_grad = pl.pallas_call(
        kernel,
        out_shape=(
            jax.ShapeDtypeStruct((96, 1024), F32),
            jax.ShapeDtypeStruct((2, 32, 1024), F32),
        ),
        in_specs=[hbm, hbm, vmem, vmem, vmem, hbm, vmem, hbm],
        out_specs=(vmem, vmem),
        scratch_shapes=scratch,
        compiler_params=pltpu.CompilerParams(
            collective_id=0, has_side_effects=True, vmem_limit_bytes=56 * 2**20
        ),
        cost_estimate=pl.CostEstimate(flops=6 * 10**9, bytes_accessed=8 * 10**6, transcendentals=0),
    )(
        teacher_hidden.reshape(8, 160, 768),
        teacher_down,
        teacher_gain.reshape(2, 4, 1, 384),
        student_stream,
        contexts,
        proj_weight,
        student_gain.reshape(1, 1024),
        head_weight.T,
    )
    head_grad, proj_grad = pl.pallas_call(
        emit,
        out_shape=(
            jax.ShapeDtypeStruct((96, 1024), F32),
            jax.ShapeDtypeStruct((2, 32, 1024), F32),
        ),
        in_specs=[vmem, vmem],
        out_specs=(hbm, hbm),
        scratch_shapes=[pltpu.SemaphoreType.DMA((2,))],
    )(head_grad, proj_grad)
    return head_grad.T, proj_grad


def solution(mesh):
    in_specs = (
        P("dp", "tensor"),
        P("tensor", None),
        P(),
        P(("dp", "tensor"), None),
        P(None, ("dp", "tensor"), None),
        P(None, "tensor", None),
        P(),
        P(None, "tensor"),
    )
    out_specs = (P(None, "tensor"), P(None, "tensor", None))
    return jax.shard_map(
        per_device, mesh=mesh, in_specs=in_specs, out_specs=out_specs, check_vma=False
    )
```

```python
import functools
import math

import jax
import jax.numpy as jnp
from jax import lax
from jax.experimental import pallas as pl
from jax.experimental.pallas import tpu as pltpu
from jax.sharding import PartitionSpec as P

MESH = pl.DeviceIdType.MESH
F32 = jnp.float32
BF16 = jnp.bfloat16
EPS = 1e-06
OWN = 40
SIDE = 64
MAIN = 160 - SIDE
SCALE = 1.0 / math.sqrt(5120)


def dot(a, b):
    return jnp.dot(a, b, preferred_element_type=F32)


def dot_nt(a, b):
    return lax.dot_general(a, b, (((1,), (1,)), ((), ())), preferred_element_type=F32)


def pack(v):
    return jnp.concatenate([v[:, 0:512], v[:, 512:1024]], axis=0).astype(BF16)


def unpack(b):
    v = b.astype(F32)
    return jnp.concatenate([v[0:OWN], v[OWN : 2 * OWN]], axis=1)


def dot_tn(a, b):
    return lax.dot_general(a, b, (((0,), (0,)), ((), ())), preferred_element_type=F32)


def kernel(
    hid, down, tgain, stream_in, ctx, pw, sgain, headt,
    hg_out, pg_out,
    hm_v, hs_v, down_v, down_b,
    msend1, mown1, mrly1, mland1, msend2, mown2, mrly2, mland2,
    ssend1, sown1, srly1, sland1, ssend2, sown2, sland2,
    xs, xr, xown,
    send3, land3,
    tsum,
    strm_s, strm_r, ctx_s, ctx_r, ctx_f,
    wk, hk,
    st_s, st_r, feat_s, feat_r, fwide,
    normed_v, istd_v, pred,
    tpad, stat, rpad, grad,
    fg, fg_s, fg_r, sg_s, sg_r, sgw,
    hx, hcr, hy, hyo, hzr, hz, hxr,
    px0, pcr0, py0, pyo0, pzr0, pz0, pxr0,
    px1, pcr1, py1, pyo1, pzr1, pz1, pxr1,
    hfin, pfin,
    lsem, ssem, rsem, tsem, usem,
):
    dp = lax.axis_index("dp")
    t = lax.axis_index("tensor")
    h, c = dp // 2, dp % 2
    xl, y, z = t // 16, (t // 4) % 4, t % 4
    xx = 2 * h + xl

    def dev(h_, c_, xl_, y_, z_):
        return {"dp": h_ * 2 + c_, "tensor": xl_ * 16 + y_ * 4 + z_}

    def dev_y(k):
        return dev(h, c, xl, (y + k) % 4, z)

    def dev_z(k):
        return dev(h, c, xl, y, (z + k) % 4)

    def dev_x(k):
        n = (xx + k) % 4
        return dev(n // 2, c, n % 2, y, z)

    xlo = dev(h, c, 1 - xl, y, z)
    xhi = dev(1 - h, c, 1 - xl, y, z)
    other = dev(h, 1 - c, xl, y, z)

    slots = [0]
    copies = []

    def send(src, dst, to):
        i = slots[0]
        slots[0] += 1
        copy = pltpu.make_async_remote_copy(
            src_ref=src, dst_ref=dst, send_sem=ssem.at[i], recv_sem=rsem.at[i],
            device_id=to, device_id_type=MESH,
        )
        copy.start()
        copies.append(copy)
        return copy

    loads = []

    def load(src, dst):
        copy = pltpu.make_async_copy(src, dst, lsem.at[len(loads)])
        copy.start()
        loads.append(copy)

    def dcol(q):
        return down.at[:, pl.ds(pl.multiple_of(384 * q, 128), 384)]

    lanes = pl.ds(pl.multiple_of(512 * c, 128), 512)
    for half in range(2):
        load(hid.at[pl.ds(4 * half, 4), pl.ds(0, MAIN)], hm_v.at[:, half])
    load(dcol((y + 2) % 4), down_v.at[2])
    load(down.at[:, pl.ds(1536, 1536)], down_b)
    for half in range(2):
        load(hid.at[pl.ds(4 * half, 4), pl.ds(MAIN, SIDE)], hs_v.at[half])
    load(pw.at[:, :, lanes], wk.at[:, xl, z, :, lanes])
    load(headt.at[:, lanes], hk.at[xl, z, :, lanes])
    for k in (1, 3, 0):
        load(dcol((y + k) % 4), down_v.at[k])

    barrier = pltpu.get_barrier_semaphore()
    for to in (
        [dev_y(k) for k in (1, 2, 3)] + [dev_z(k) for k in (1, 2, 3)]
        + [dev_x(k) for k in (1, 2, 3)] + [other]
    ):
        pl.semaphore_signal(barrier, 1, device_id=to, device_id_type=MESH)
    for j in range(4):
        mine = jnp.where(jnp.logical_and(y == z, z == j), 1, 0)
        to = dev(h, c + mine * (1 - 2 * c), xl, z, j)
        pl.semaphore_signal(barrier, 1, device_id=to, device_id_type=MESH)

    tpad[...] = jnp.zeros_like(tpad)
    rpad[...] = jnp.zeros_like(rpad)

    def main_product(ab, k):
        if ab == 0:
            value = dot(hm_v[...].reshape(8 * MAIN, 768), down_v[k]).reshape(4, 2 * MAIN, 384)
            if k == 0:
                mown1[0] = value
            else:
                msend1[0, k - 1] = value.astype(BF16)
            return

        value = dot(hm_v[(z + k) % 4].reshape(2 * MAIN, 768), down_b[...])
        for i in range(4):
            block = value[:, 384 * i : 384 * i + 384]
            if k == 0:
                mown1[1, i] = block
            else:
                msend1[1, k - 1, i] = block.astype(BF16)

    def side_product_y(k, rows, out):
        out[0, k] = dot(hs_v[rows].reshape(4 * SIDE, 768), down_v[k]).reshape(4, SIDE, 384).astype(out.dtype)

    def side_product_z(rows, out):
        value = dot(hs_v[rows].reshape(4 * SIDE, 768), down_b[...]).reshape(4, SIDE, 1536).astype(out.dtype)
        for q in range(4):
            for i in range(4):
                out[1, (q - z + 4) % 4, i] = value[q, :, 384 * i : 384 * i + 384]

    class Ring:
        def __init__(self, to, ab, n, sbuf, rly, land):
            self.to, self.ab, self.n, self.m = to, ab, n, n // 2
            self.sbuf, self.rly, self.land = sbuf, rly, land
            self.relays, self.final = [], []

        def halves(self):
            return pl.ds(0, self.m), pl.ds(self.m, self.n - self.m)

        def relay_out(self):
            low, high = self.halves()
            for d, part in ((0, low), (1, high)):
                self.relays.append(
                    send(self.sbuf.at[self.ab, 1, part], self.rly.at[self.ab, d, part], self.to(1 + 2 * d))
                )

        def direct_out(self, k):
            low, high = self.halves()
            d, part = (0, high) if k == 1 else (1, low)
            self.final.append(
                send(self.sbuf.at[self.ab, k - 1, part], self.land.at[self.ab, d, part], self.to(k))
            )

        def relay_on(self):
            low, high = self.halves()
            for d, k, part, slabs in (
                (0, 1, low, range(self.m)),
                (1, 3, high, range(self.m, self.n)),
            ):
                self.relays[d].wait_recv()
                for i in slabs:
                    value = self.sbuf[self.ab, k - 1, i].astype(F32) + self.rly[self.ab, d, i].astype(F32)
                    self.sbuf[self.ab, k - 1, i] = value.astype(BF16)
                self.final.append(
                    send(self.sbuf.at[self.ab, k - 1, part], self.land.at[self.ab, d, part], self.to(k))
                )

        def finish(self):
            for w in self.final:
                w.wait_recv()

    main1 = [Ring(dev_y, 0, 4, msend1, mrly1, mland1), Ring(dev_z, 1, 4, msend1, mrly1, mland1)]
    main2 = [Ring(dev_z, 0, 2, msend2, mrly2, mland2), Ring(dev_y, 1, 2, msend2, mrly2, mland2)]
    side1 = [Ring(dev_y, 0, 4, ssend1, srly1, sland1), Ring(dev_z, 1, 4, ssend1, srly1, sland1)]

    for i in range(3):
        loads[i].wait()
    main_product(0, 2)
    pl.semaphore_wait(barrier, 14)
    main1[0].relay_out()
    for i in range(3, 6):
        loads[i].wait()
    main_product(1, 2)
    main1[1].relay_out()
    xc = [[None] * 4, [None] * 4]

    def x_first(ab, k):
        xc[ab][k] = send(xs.at[ab, k], xr.at[ab, k], xlo)

    side_product_y(2, 1 - xl, xs)
    x_first(0, 2)

    strm_s[...] = pack(stream_in[...].astype(F32))
    for q in range(4):
        parts = [
            ctx[layer, :, 512 * half + 128 * q : 512 * half + 128 * q + 128].astype(F32)
            for layer in range(2)
            for half in range(2)
        ]
        ctx_s[q] = jnp.concatenate(parts, axis=0).astype(BF16)
    strm_self = jnp.logical_and(y == z, z == y)
    strm_to = pltpu.make_async_remote_copy(
        src_ref=strm_s, dst_ref=strm_r, send_sem=usem.at[8], recv_sem=usem.at[9],
        device_id=dev(h, c, xl, z, y), device_id_type=MESH,
    )

    @pl.when(strm_self)
    def _():
        pltpu.make_async_copy(strm_s, strm_r, usem.at[9]).start()

    @pl.when(jnp.logical_not(strm_self))
    def _():
        strm_to.start()

    ctx_to = []
    for q in range(4):
        mine = jnp.logical_and(y == z, y == q)
        copy = pltpu.make_async_remote_copy(
            src_ref=ctx_s.at[q], dst_ref=ctx_r.at[z], send_sem=usem.at[q], recv_sem=tsem.at[z],
            device_id=dev(h, c, xl, q, y), device_id_type=MESH,
        )
        ctx_to.append((mine, copy))

        @pl.when(mine)
        def _():
            pltpu.make_async_copy(ctx_s.at[q], ctx_r.at[z], tsem.at[z]).start()

        @pl.when(jnp.logical_not(mine))
        def _():
            copy.start()

    loads[6].wait()
    wz_c = [send(wk.at[:, xl, z, :, lanes], wk.at[:, xl, z, :, lanes], dev_z(k)) for k in (2, 1, 3)]
    side_product_z(1 - xl, xs)
    x_first(1, 2)
    for i in range(7, 11):
        loads[i].wait()
    for ab in range(2):
        for k in (1, 3):
            main_product(ab, k)
            main1[ab].direct_out(k)
    for k in (1, 3, 0):
        side_product_y(k, 1 - xl, xs)
        x_first(0, k)
        x_first(1, k)
    main_product(0, 0)
    main_product(1, 0)
    for k in (2, 1, 3, 0):
        side_product_y(k, xl, xown)
    side_product_z(xl, xown)
    for ab in range(2):
        main1[ab].relay_on()
    hz_c = [send(hk.at[xl, z, :, lanes], hk.at[xl, z, :, lanes], dev_z(k)) for k in (2, 1, 3)]

    def side_add(ab, k):
        xc[ab][k].wait_recv()
        value = xown[ab, k] + xr[ab, k].astype(F32)
        if k == 0:
            sown1[ab] = value
        else:
            ssend1[ab, k - 1] = value.astype(BF16)

    for ab in range(2):
        side_add(ab, 2)
        side1[ab].relay_out()
    for w in wz_c:
        w.wait_recv()
    wx_c = [send(wk.at[:, xl, :, :, lanes], wk.at[:, xl, :, :, lanes], xhi)]
    for ab in range(2):
        side_add(ab, 1)
        side1[ab].direct_out(1)

    for j in range(4):
        pltpu.make_async_remote_copy(
            src_ref=ctx_s.at[j], dst_ref=ctx_r.at[j], send_sem=usem.at[j], recv_sem=tsem.at[j],
            device_id=dev(h, c, xl, j, y), device_id_type=MESH,
        ).wait_recv()
        block = ctx_r[j].astype(F32)
        for i in range(4):
            ctx_f[OWN * j : OWN * j + OWN, 128 * i : 128 * i + 128] = block[OWN * i : OWN * i + OWN]
    wx_c[0].wait_recv()
    wc_c = [send(wk.at[:, :, :, :, lanes], wk.at[:, :, :, :, lanes], other)]
    wc_c[0].wait_recv()
    fg[...] = dot(ctx_f[...].astype(BF16), wk[...].reshape(512, 1024)).reshape(4, OWN, 1024)
    for k in (2, 1, 3):
        st_s[k - 1] = pack(fg[(y + k) % 4])
    st_c = [send(st_s.at[k - 1], st_r.at[k - 1], dev_y(k)) for k in (2, 1, 3)]

    def total1(own1, land1, ab, k):
        q = ((z if ab == 0 else y) + k) % 4
        return own1[ab, q] + land1[ab, 0, q].astype(F32) + land1[ab, 1, q].astype(F32)

    def main_second(ab):
        main1[ab].finish()
        for k in (2, 1, 3, 0):
            value = total1(mown1, mland1, ab, k).reshape(2, MAIN, 384)
            if k == 0:
                mown2[ab] = value
                continue
            msend2[ab, k - 1] = value.astype(BF16)
            if k == 2:
                main2[ab].relay_out()
            else:
                main2[ab].direct_out(k)

    def side_second(ab):
        side1[ab].finish()
        out = []
        for k in (2, 1, 3, 0):
            value = total1(sown1, sland1, ab, k)
            if k == 0:
                sown2[ab] = value
                continue
            ssend2[ab, k - 1] = value.astype(BF16)
            to = dev_z(k) if ab == 0 else dev_y(k)
            out.append(send(ssend2.at[ab, k - 1], sland2.at[ab, k - 1], to))
        return out

    side_add(0, 3)
    side1[0].direct_out(3)
    side1[0].relay_on()
    main_second(0)
    side_add(1, 3)
    side1[1].direct_out(3)
    side1[1].relay_on()
    main_second(1)
    for w in hz_c:
        w.wait_recv()
    wx_c.append(send(hk.at[xl, :, :, lanes], hk.at[xl, :, :, lanes], xhi))
    main2[0].relay_on()
    main2[1].relay_on()
    side2 = []
    for ab in range(2):
        side_add(ab, 0)
        side2.append(side_second(ab))
    def main_total(ab, q):
        return mown2[ab, q] + mland2[ab, 0, q].astype(F32) + mland2[ab, 1, q].astype(F32)

    x3 = []
    for ab in range(2):
        main2[ab].finish()
        send3[ab] = main_total(ab, 1 - xl).astype(BF16)
        x3.append(send(send3.at[ab], land3.at[ab], xlo))
    strm_to.wait_recv()
    stream = unpack(strm_r[...]) + fg[y]
    for w in st_c:
        w.wait_recv()
    for k in range(3):
        stream = stream + unpack(st_r[k])
    centered = stream - jnp.mean(stream, axis=-1, keepdims=True)
    istd = lax.rsqrt(jnp.mean(centered * centered, axis=-1, keepdims=True) + EPS)
    normed = centered * istd
    normed_v[...] = normed
    istd_v[...] = jnp.broadcast_to(istd, istd_v.shape)
    feat_s[...] = pack(normed * sgain[...])
    ft_c = [send(feat_s, feat_r.at[y], dev_y(k)) for k in (2, 1, 3)]
    feat_r[y] = feat_s[...]

    wx_c[1].wait_recv()
    wc_c.append(send(hk.at[:, :, :, lanes], hk.at[:, :, :, lanes], other))

    for ab in range(2):
        s = slice(384 * ab, 384 * ab + 384)
        for w in side2[ab]:
            w.wait_recv()
        value = sown2[ab]
        for k in range(3):
            value = value + sland2[ab, k].astype(F32)
        tsum[MAIN:160, s] = value
        x3[ab].wait_recv()
        tsum[0:MAIN, s] = main_total(ab, xl) + land3[ab].astype(F32)

    teach = tsum[...]
    mean_own = jnp.mean(teach, axis=-1, keepdims=True)
    cent = teach - mean_own
    m2_own = jnp.sum(cent * cent, axis=-1, keepdims=True)
    lane = lax.broadcasted_iota(jnp.int32, (160, 128), 1)
    tpad[0:160, :] = jnp.where(lane == 0, mean_own, jnp.where(lane == 1, m2_own, 0.0))
    stat[0] = tpad[...].T[0:8, :]
    sc = [send(stat.at[0], stat.at[k], dev_y(k)) for k in (2, 1, 3)]

    for w in ft_c:
        w.wait_recv()
    for q in range(4):
        fwide[OWN * q : OWN * q + OWN, :] = unpack(feat_r[q])
    feats = fwide[...].astype(BF16)
    wc_c[1].wait_recv()
    pred[...] = dot_nt(feats, hk[...].reshape(768, 1024))
    for w in sc:
        w.wait_recv()
    means = [stat[k, 0:1, :] for k in range(4)]
    mean_row = (means[0] + means[1] + means[2] + means[3]) * 0.25
    m2_row = sum(stat[k, 1:2, :] for k in range(4)) + 768.0 * sum((m - mean_row) ** 2 for m in means)
    rpad[0:1, :] = mean_row
    rpad[1:2, :] = lax.rsqrt(m2_row * (1.0 / 3072) + EPS)
    cols = rpad[...].T
    mean_col, istd_col = cols[0:160, 0:1], cols[0:160, 1:2]
    for half in range(2):
        s = slice(384 * half, 384 * half + 384)
        target = ((tsum[:, s] - mean_col) * istd_col * tgain[half, y]).astype(BF16)
        grad[:, s] = ((pred[:, s] - target.astype(F32)) * SCALE).astype(BF16)

    grads = grad[...]
    fg[...] = dot(grads, hk[...].reshape(768, 1024)).reshape(4, OWN, 1024)
    for k in (2, 1, 3):
        fg_s[k - 1] = pack(fg[(y + k) % 4])
    fg_c = [send(fg_s.at[k - 1], fg_r.at[k - 1], dev_y(k)) for k in (2, 1, 3)]

    hgt = dot_tn(grads, feats).astype(BF16)
    for half in range(2):
        hx[half] = hgt[:, 512 * half : 512 * half + 512].reshape(2, 4, 96, 512)

    def core_out(xbuf, crbuf):
        return send(xbuf.at[1 - c], crbuf, other)

    def z_out(xbuf, crbuf, ybuf, yown, zrbuf, arrival):
        arrival.wait_recv()
        out = []
        for k in (2, 1, 3, 0):
            q = (z + k) % 4
            value = xbuf[c, :, q].astype(F32) + crbuf[:, q].astype(F32)
            if k == 0:
                yown[...] = value
            else:
                ybuf[k - 1] = value.astype(BF16)
                out.append(send(ybuf.at[k - 1], zrbuf.at[k - 1], dev_z(k)))
        return out

    def x_out(yown, zrbuf, zbuf, xrbuf, arrivals):
        for w in arrivals:
            w.wait_recv()
        value = yown[...] + zrbuf[0].astype(F32) + zrbuf[1].astype(F32) + zrbuf[2].astype(F32)
        zbuf[...] = value.astype(BF16)
        out = [
            send(zbuf.at[1 - xl if k % 2 else xl], xrbuf.at[xx], dev_x(k)) for k in (2, 1, 3)
        ]
        xrbuf[xx] = zbuf[xl]
        return out

    def last(xrbuf, fin, arrivals):
        for w in arrivals:
            w.wait_recv()
        fin[c] = (xrbuf[0].astype(F32) + xrbuf[1].astype(F32)) + (xrbuf[2].astype(F32) + xrbuf[3].astype(F32))
        return send(fin.at[c], fin.at[c], other)

    hc_c = core_out(hx, hcr)

    hzc = z_out(hx, hcr, hy, hyo, hzr, hc_c)

    gsum = fg[y]
    for w in fg_c:
        w.wait_recv()
    for k in range(3):
        gsum = gsum + unpack(fg_r[k])
    weighted = gsum * sgain[...]
    nrm = normed_v[...]
    first = jnp.mean(weighted, axis=-1, keepdims=True)
    second = jnp.mean(weighted * nrm, axis=-1, keepdims=True)
    sg_s[...] = pack(istd_v[:, 0:1] * (weighted - first - nrm * second))
    sg_c = [send(sg_s, sg_r.at[y], dev_y(k)) for k in (2, 1, 3)]
    sg_r[y] = sg_s[...]

    for w in sg_c:
        w.wait_recv()
    for q in range(4):
        sgw[OWN * q : OWN * q + OWN, :] = unpack(sg_r[q])
    sgrads = sgw[...].astype(BF16)
    pbufs = (
        (px0, pcr0, py0, pyo0, pzr0, pz0, pxr0),
        (px1, pcr1, py1, pyo1, pzr1, pz1, pxr1),
    )
    pc_c = []
    for layer in range(2):
        px = pbufs[layer][0]
        for half in range(2):
            j = 2 * layer + half
            block = ctx_f[:, 128 * j : 128 * j + 128].astype(BF16)
            value = dot_tn(block, sgrads).astype(BF16)
            for s in range(2):
                px[s, half] = value[:, 512 * s : 512 * s + 512].reshape(4, 32, 512)
        pc_c.append(core_out(px, pbufs[layer][1]))
    pzc = []
    for layer in range(2):
        px, pcr, py, pyo, pzr, pz, pxr = pbufs[layer]
        pzc.append(z_out(px, pcr, py, pyo, pzr, pc_c[layer]))
    hxc = x_out(hyo, hzr, hz, hxr, hzc)
    pxc = []
    for layer in range(2):
        px, pcr, py, pyo, pzr, pz, pxr = pbufs[layer]
        pxc.append(x_out(pyo, pzr, pz, pxr, pzc[layer]))
    hlast = last(hxr, hfin, hxc)
    plast = [last(pbufs[layer][6], pfin.at[layer], pxc[layer]) for layer in range(2)]
    hlast.wait_recv()
    for s in range(2):
        hg_out[:, 512 * s : 512 * s + 512] = hfin[s]
    for layer in range(2):
        plast[layer].wait_recv()
        for s in range(2):
            pg_out[layer, :, 512 * s : 512 * s + 512] = pfin[layer, s]
    for copy in copies:
        copy.wait_send()

    @pl.when(jnp.logical_not(strm_self))
    def _():
        strm_to.wait_send()

    for mine, copy in ctx_to:

        @pl.when(jnp.logical_not(mine))
        def _():
            copy.wait_send()

    assert slots[0] <= N_SLOTS


N_SLOTS = 128


def emit(hg_in, pg_in, hg_out, pg_out, sem):
    copies = [
        pltpu.make_async_copy(hg_in, hg_out, sem.at[0]),
        pltpu.make_async_copy(pg_in, pg_out, sem.at[1]),
    ]
    for copy in copies:
        copy.start()
    for copy in copies:
        copy.wait()


def per_device(
    teacher_hidden, teacher_down, teacher_gain, student_stream, contexts, proj_weight, student_gain, head_weight
):
    vmem = pl.BlockSpec(memory_space=pltpu.VMEM)
    hbm = pl.BlockSpec(memory_space=pl.ANY)

    def v(*shape, dtype=BF16):
        return pltpu.VMEM(shape, dtype)

    def reduce_bufs(tail):
        return [
            v(2, 2, 4, *tail), v(2, 4, *tail), v(3, 2, *tail), v(2, *tail, dtype=F32),
            v(3, 2, *tail), v(2, *tail), v(4, *tail),
        ]

    def ring_bufs(rows):
        return [v(2, 3, 4, rows, 384), v(2, 4, rows, 384, dtype=F32), v(2, 2, 4, rows, 384), v(2, 2, 4, rows, 384)]

    scratch = [
        v(4, 2, MAIN, 768), v(2, 4, SIDE, 768), v(4, 768, 384), v(768, 1536),
        *ring_bufs(2 * MAIN),
        v(2, 3, 2, MAIN, 384), v(2, 2, MAIN, 384, dtype=F32), v(2, 2, 2, MAIN, 384), v(2, 2, 2, MAIN, 384),
        *ring_bufs(SIDE),
        v(2, 3, SIDE, 384), v(2, SIDE, 384, dtype=F32), v(2, 3, SIDE, 384),
        v(2, 4, 4, SIDE, 384), v(2, 4, 4, SIDE, 384), v(2, 4, 4, SIDE, 384, dtype=F32),
        v(2, MAIN, 384), v(2, MAIN, 384),
        v(160, 768, dtype=F32),
        v(80, 512), v(80, 512), v(4, 160, 128), v(4, 160, 128), v(160, 512, dtype=F32),
        v(2, 2, 4, 32, 1024), v(2, 4, 96, 1024),
        v(3, 80, 512), v(3, 80, 512), v(80, 512), v(4, 80, 512), v(160, 1024, dtype=F32),
        v(OWN, 1024, dtype=F32), v(OWN, 128, dtype=F32), v(160, 768, dtype=F32),
        v(256, 128, dtype=F32), v(4, 8, 256, dtype=F32), v(128, 256, dtype=F32), v(160, 768),
        v(4, OWN, 1024, dtype=F32), v(3, 80, 512), v(3, 80, 512), v(80, 512), v(4, 80, 512),
        v(160, 1024, dtype=F32),
        *reduce_bufs((96, 512)),
        *reduce_bufs((32, 512)),
        *reduce_bufs((32, 512)),
        v(2, 96, 512, dtype=F32), v(2, 2, 32, 512, dtype=F32),
        pltpu.SemaphoreType.DMA((16,)), pltpu.SemaphoreType.DMA((N_SLOTS,)), pltpu.SemaphoreType.DMA((N_SLOTS,)),
        pltpu.SemaphoreType.DMA((4,)), pltpu.SemaphoreType.DMA((10,)),
    ]
    head_grad, proj_grad = pl.pallas_call(
        kernel,
        out_shape=(
            jax.ShapeDtypeStruct((96, 1024), F32),
            jax.ShapeDtypeStruct((2, 32, 1024), F32),
        ),
        in_specs=[hbm, hbm, vmem, vmem, vmem, hbm, vmem, hbm],
        out_specs=(vmem, vmem),
        scratch_shapes=scratch,
        compiler_params=pltpu.CompilerParams(
            collective_id=0, has_side_effects=True, vmem_limit_bytes=56 * 2**20
        ),
        cost_estimate=pl.CostEstimate(flops=6 * 10**9, bytes_accessed=8 * 10**6, transcendentals=0),
    )(
        teacher_hidden.reshape(8, 160, 768),
        teacher_down,
        teacher_gain.reshape(2, 4, 1, 384),
        student_stream,
        contexts,
        proj_weight,
        student_gain.reshape(1, 1024),
        head_weight.T,
    )
    head_grad, proj_grad = pl.pallas_call(
        emit,
        out_shape=(
            jax.ShapeDtypeStruct((96, 1024), F32),
            jax.ShapeDtypeStruct((2, 32, 1024), F32),
        ),
        in_specs=[vmem, vmem],
        out_specs=(hbm, hbm),
        scratch_shapes=[pltpu.SemaphoreType.DMA((2,))],
    )(head_grad, proj_grad)
    return head_grad.T, proj_grad


def solution(mesh):
    in_specs = (
        P("dp", "tensor"),
        P("tensor", None),
        P(),
        P(("dp", "tensor"), None),
        P(None, ("dp", "tensor"), None),
        P(None, "tensor", None),
        P(),
        P(None, "tensor"),
    )
    out_specs = (P(None, "tensor"), P(None, "tensor", None))
    return jax.shard_map(
        per_device, mesh=mesh, in_specs=in_specs, out_specs=out_specs, check_vma=False
    )
```

```python
import functools
import math

import jax
import jax.numpy as jnp
from jax import lax
from jax.experimental import pallas as pl
from jax.experimental.pallas import tpu as pltpu
from jax.sharding import PartitionSpec as P

MESH = pl.DeviceIdType.MESH
F32 = jnp.float32
BF16 = jnp.bfloat16
EPS = 1e-06
OWN = 40
SIDE = 64
MAIN = 160 - SIDE
SCALE = 1.0 / math.sqrt(5120)


def dot(a, b):
    return jnp.dot(a, b, preferred_element_type=F32)


def dot_nt(a, b):
    return lax.dot_general(a, b, (((1,), (1,)), ((), ())), preferred_element_type=F32)


def pack(v):
    return jnp.concatenate([v[:, 0:512], v[:, 512:1024]], axis=0).astype(BF16)


def unpack(b):
    v = b.astype(F32)
    return jnp.concatenate([v[0:OWN], v[OWN : 2 * OWN]], axis=1)


def dot_tn(a, b):
    return lax.dot_general(a, b, (((0,), (0,)), ((), ())), preferred_element_type=F32)


def kernel(
    hid, down, tgain, stream_in, ctx, pw, sgain, headt,
    hg_out, pg_out,
    hm_v, hs_v, down_v, down_b,
    msend1, mown1, mrly1, mland1, msend2, mown2, mrly2, mland2,
    ssend1, sown1, srly1, sland1, ssend2, sown2, sland2,
    xs, xr, xown,
    send3, land3,
    tsum,
    strm_s, strm_r, ctx_s, ctx_r, ctx_f,
    wk, hk,
    st_s, st_r, feat_s, feat_r, fwide,
    normed_v, istd_v, pred,
    tpad, stat, rpad, grad,
    fg, fg_s, fg_r, sg_s, sg_r, sgw,
    hx, hcr, hy, hyo, hzr, hz, hxr,
    px0, pcr0, py0, pyo0, pzr0, pz0, pxr0,
    px1, pcr1, py1, pyo1, pzr1, pz1, pxr1,
    hfin, pfin,
    lsem, ssem, rsem, tsem, usem,
):
    dp = lax.axis_index("dp")
    t = lax.axis_index("tensor")
    h, c = dp // 2, dp % 2
    xl, y, z = t // 16, (t // 4) % 4, t % 4
    xx = 2 * h + xl

    def dev(h_, c_, xl_, y_, z_):
        return {"dp": h_ * 2 + c_, "tensor": xl_ * 16 + y_ * 4 + z_}

    def dev_y(k):
        return dev(h, c, xl, (y + k) % 4, z)

    def dev_z(k):
        return dev(h, c, xl, y, (z + k) % 4)

    def dev_x(k):
        n = (xx + k) % 4
        return dev(n // 2, c, n % 2, y, z)

    xlo = dev(h, c, 1 - xl, y, z)
    xhi = dev(1 - h, c, 1 - xl, y, z)
    other = dev(h, 1 - c, xl, y, z)

    slots = [0]
    copies = []

    def send(src, dst, to):
        i = slots[0]
        slots[0] += 1
        copy = pltpu.make_async_remote_copy(
            src_ref=src, dst_ref=dst, send_sem=ssem.at[i], recv_sem=rsem.at[i],
            device_id=to, device_id_type=MESH,
        )
        copy.start()
        copies.append(copy)
        return copy

    loads = []

    def load(src, dst):
        copy = pltpu.make_async_copy(src, dst, lsem.at[len(loads)])
        copy.start()
        loads.append(copy)

    def dcol(q):
        return down.at[:, pl.ds(pl.multiple_of(384 * q, 128), 384)]

    lanes = pl.ds(pl.multiple_of(512 * c, 128), 512)
    for half in range(2):
        load(hid.at[pl.ds(4 * half, 4), pl.ds(0, MAIN)], hm_v.at[:, half])
    load(dcol((y + 2) % 4), down_v.at[2])
    load(down.at[:, pl.ds(1536, 1536)], down_b)
    for half in range(2):
        load(hid.at[pl.ds(4 * half, 4), pl.ds(MAIN, SIDE)], hs_v.at[half])
    load(pw.at[:, :, lanes], wk.at[:, xl, z, :, lanes])
    load(headt.at[:, lanes], hk.at[xl, z, :, lanes])
    for k in (1, 3, 0):
        load(dcol((y + k) % 4), down_v.at[k])

    barrier = pltpu.get_barrier_semaphore()
    for to in (
        [dev_y(k) for k in (1, 2, 3)] + [dev_z(k) for k in (1, 2, 3)]
        + [dev_x(k) for k in (1, 2, 3)] + [other]
    ):
        pl.semaphore_signal(barrier, 1, device_id=to, device_id_type=MESH)
    for j in range(4):
        mine = jnp.where(jnp.logical_and(y == z, z == j), 1, 0)
        to = dev(h, c + mine * (1 - 2 * c), xl, z, j)
        pl.semaphore_signal(barrier, 1, device_id=to, device_id_type=MESH)

    tpad[...] = jnp.zeros_like(tpad)
    rpad[...] = jnp.zeros_like(rpad)

    def main_product(ab, k):
        if ab == 0:
            value = dot(hm_v[...].reshape(8 * MAIN, 768), down_v[k]).reshape(4, 2 * MAIN, 384)
            if k == 0:
                mown1[0] = value
            else:
                msend1[0, k - 1] = value.astype(BF16)
            return

        value = dot(hm_v[(z + k) % 4].reshape(2 * MAIN, 768), down_b[...])
        for i in range(4):
            block = value[:, 384 * i : 384 * i + 384]
            if k == 0:
                mown1[1, i] = block
            else:
                msend1[1, k - 1, i] = block.astype(BF16)

    def side_product_y(k, rows, out):
        out[0, k] = dot(hs_v[rows].reshape(4 * SIDE, 768), down_v[k]).reshape(4, SIDE, 384).astype(out.dtype)

    def side_product_z(rows, out):
        value = dot(hs_v[rows].reshape(4 * SIDE, 768), down_b[...]).reshape(4, SIDE, 1536).astype(out.dtype)
        for q in range(4):
            for i in range(4):
                out[1, (q - z + 4) % 4, i] = value[q, :, 384 * i : 384 * i + 384]

    class Ring:
        def __init__(self, to, ab, n, sbuf, rly, land):
            self.to, self.ab, self.n, self.m = to, ab, n, n // 2
            self.sbuf, self.rly, self.land = sbuf, rly, land
            self.relays, self.final = [], []

        def halves(self):
            return pl.ds(0, self.m), pl.ds(self.m, self.n - self.m)

        def relay_out(self):
            low, high = self.halves()
            for d, part in ((0, low), (1, high)):
                self.relays.append(
                    send(self.sbuf.at[self.ab, 1, part], self.rly.at[self.ab, d, part], self.to(1 + 2 * d))
                )

        def direct_out(self, k):
            low, high = self.halves()
            d, part = (0, high) if k == 1 else (1, low)
            self.final.append(
                send(self.sbuf.at[self.ab, k - 1, part], self.land.at[self.ab, d, part], self.to(k))
            )

        def relay_on(self):
            low, high = self.halves()
            for d, k, part, slabs in (
                (0, 1, low, range(self.m)),
                (1, 3, high, range(self.m, self.n)),
            ):
                self.relays[d].wait_recv()
                for i in slabs:
                    value = self.sbuf[self.ab, k - 1, i].astype(F32) + self.rly[self.ab, d, i].astype(F32)
                    self.sbuf[self.ab, k - 1, i] = value.astype(BF16)
                self.final.append(
                    send(self.sbuf.at[self.ab, k - 1, part], self.land.at[self.ab, d, part], self.to(k))
                )

        def finish(self):
            for w in self.final:
                w.wait_recv()

    main1 = [Ring(dev_y, 0, 4, msend1, mrly1, mland1), Ring(dev_z, 1, 4, msend1, mrly1, mland1)]
    main2 = [Ring(dev_z, 0, 2, msend2, mrly2, mland2), Ring(dev_y, 1, 2, msend2, mrly2, mland2)]
    side1 = [Ring(dev_y, 0, 4, ssend1, srly1, sland1), Ring(dev_z, 1, 4, ssend1, srly1, sland1)]

    strm_s[...] = pack(stream_in[...].astype(F32))
    for q in range(4):
        parts = [
            ctx[layer, :, 512 * half + 128 * q : 512 * half + 128 * q + 128].astype(F32)
            for layer in range(2)
            for half in range(2)
        ]
        ctx_s[q] = jnp.concatenate(parts, axis=0).astype(BF16)
    pl.semaphore_wait(barrier, 14)
    strm_self = jnp.logical_and(y == z, z == y)
    strm_to = pltpu.make_async_remote_copy(
        src_ref=strm_s, dst_ref=strm_r, send_sem=usem.at[8], recv_sem=usem.at[9],
        device_id=dev(h, c, xl, z, y), device_id_type=MESH,
    )

    @pl.when(strm_self)
    def _():
        pltpu.make_async_copy(strm_s, strm_r, usem.at[9]).start()

    @pl.when(jnp.logical_not(strm_self))
    def _():
        strm_to.start()

    ctx_to = []
    for q in range(4):
        mine = jnp.logical_and(y == z, y == q)
        copy = pltpu.make_async_remote_copy(
            src_ref=ctx_s.at[q], dst_ref=ctx_r.at[z], send_sem=usem.at[q], recv_sem=tsem.at[z],
            device_id=dev(h, c, xl, q, y), device_id_type=MESH,
        )
        ctx_to.append((mine, copy))

        @pl.when(mine)
        def _():
            pltpu.make_async_copy(ctx_s.at[q], ctx_r.at[z], tsem.at[z]).start()

        @pl.when(jnp.logical_not(mine))
        def _():
            copy.start()

    loads[6].wait()
    wz_c = [send(wk.at[:, xl, z, :, lanes], wk.at[:, xl, z, :, lanes], dev_z(k)) for k in (2, 1, 3)]
    for i in range(3):
        loads[i].wait()
    main_product(0, 2)
    main1[0].relay_out()
    for i in range(3, 6):
        loads[i].wait()
    main_product(1, 2)
    main1[1].relay_out()
    loads[7].wait()
    hz_c = [send(hk.at[xl, z, :, lanes], hk.at[xl, z, :, lanes], dev_z(k)) for k in (2, 1, 3)]
    xc = [[None] * 4, [None] * 4]

    def x_first(ab, k):
        xc[ab][k] = send(xs.at[ab, k], xr.at[ab, k], xlo)

    side_product_y(2, 1 - xl, xs)
    x_first(0, 2)

    side_product_z(1 - xl, xs)
    x_first(1, 2)
    for i in range(8, 11):
        loads[i].wait()
    for ab in range(2):
        for k in (1, 3):
            main_product(ab, k)
            main1[ab].direct_out(k)
    for k in (1, 3, 0):
        side_product_y(k, 1 - xl, xs)
        x_first(0, k)
        x_first(1, k)
    for w in wz_c:
        w.wait_recv()
    wx_c = [send(wk.at[:, xl, :, :, lanes], wk.at[:, xl, :, :, lanes], xhi)]
    main_product(0, 0)
    main_product(1, 0)
    for k in (2, 1, 3, 0):
        side_product_y(k, xl, xown)
    side_product_z(xl, xown)
    for ab in range(2):
        main1[ab].relay_on()

    def side_add(ab, k):
        xc[ab][k].wait_recv()
        value = xown[ab, k] + xr[ab, k].astype(F32)
        if k == 0:
            sown1[ab] = value
        else:
            ssend1[ab, k - 1] = value.astype(BF16)

    for ab in range(2):
        side_add(ab, 2)
        side1[ab].relay_out()
    for j in range(4):
        pltpu.make_async_remote_copy(
            src_ref=ctx_s.at[j], dst_ref=ctx_r.at[j], send_sem=usem.at[j], recv_sem=tsem.at[j],
            device_id=dev(h, c, xl, j, y), device_id_type=MESH,
        ).wait_recv()
        block = ctx_r[j].astype(F32)
        for i in range(4):
            ctx_f[OWN * j : OWN * j + OWN, 128 * i : 128 * i + 128] = block[OWN * i : OWN * i + OWN]
    wx_c[0].wait_recv()
    wc_c = [send(wk.at[:, :, :, :, lanes], wk.at[:, :, :, :, lanes], other)]
    wc_c[0].wait_recv()
    fg[...] = dot(ctx_f[...].astype(BF16), wk[...].reshape(512, 1024)).reshape(4, OWN, 1024)
    for k in (2, 1, 3):
        st_s[k - 1] = pack(fg[(y + k) % 4])
    st_c = [send(st_s.at[k - 1], st_r.at[k - 1], dev_y(k)) for k in (2, 1, 3)]
    for w in hz_c:
        w.wait_recv()
    wx_c.append(send(hk.at[xl, :, :, lanes], hk.at[xl, :, :, lanes], xhi))
    for ab in range(2):
        side_add(ab, 1)
        side1[ab].direct_out(1)


    def total1(own1, land1, ab, k):
        q = ((z if ab == 0 else y) + k) % 4
        return own1[ab, q] + land1[ab, 0, q].astype(F32) + land1[ab, 1, q].astype(F32)

    def main_second(ab):
        main1[ab].finish()
        for k in (2, 1, 3, 0):
            value = total1(mown1, mland1, ab, k).reshape(2, MAIN, 384)
            if k == 0:
                mown2[ab] = value
                continue
            msend2[ab, k - 1] = value.astype(BF16)
            if k == 2:
                main2[ab].relay_out()
            else:
                main2[ab].direct_out(k)

    def side_second(ab):
        side1[ab].finish()
        out = []
        for k in (2, 1, 3, 0):
            value = total1(sown1, sland1, ab, k)
            if k == 0:
                sown2[ab] = value
                continue
            ssend2[ab, k - 1] = value.astype(BF16)
            to = dev_z(k) if ab == 0 else dev_y(k)
            out.append(send(ssend2.at[ab, k - 1], sland2.at[ab, k - 1], to))
        return out

    side_add(0, 3)
    side1[0].direct_out(3)
    side1[0].relay_on()
    main_second(0)
    side_add(1, 3)
    side1[1].direct_out(3)
    side1[1].relay_on()
    main_second(1)
    strm_to.wait_recv()
    stream = unpack(strm_r[...]) + fg[y]
    for w in st_c:
        w.wait_recv()
    for k in range(3):
        stream = stream + unpack(st_r[k])
    centered = stream - jnp.mean(stream, axis=-1, keepdims=True)
    istd = lax.rsqrt(jnp.mean(centered * centered, axis=-1, keepdims=True) + EPS)
    normed = centered * istd
    normed_v[...] = normed
    istd_v[...] = jnp.broadcast_to(istd, istd_v.shape)
    feat_s[...] = pack(normed * sgain[...])
    ft_c = [send(feat_s, feat_r.at[y], dev_y(k)) for k in (2, 1, 3)]
    feat_r[y] = feat_s[...]
    wx_c[1].wait_recv()
    wc_c.append(send(hk.at[:, :, :, lanes], hk.at[:, :, :, lanes], other))
    main2[0].relay_on()
    main2[1].relay_on()
    side2 = []
    for ab in range(2):
        side_add(ab, 0)
        side2.append(side_second(ab))
    def main_total(ab, q):
        return mown2[ab, q] + mland2[ab, 0, q].astype(F32) + mland2[ab, 1, q].astype(F32)

    x3 = []
    for ab in range(2):
        main2[ab].finish()
        send3[ab] = main_total(ab, 1 - xl).astype(BF16)
        x3.append(send(send3.at[ab], land3.at[ab], xlo))


    for ab in range(2):
        s = slice(384 * ab, 384 * ab + 384)
        for w in side2[ab]:
            w.wait_recv()
        value = sown2[ab]
        for k in range(3):
            value = value + sland2[ab, k].astype(F32)
        tsum[MAIN:160, s] = value
        x3[ab].wait_recv()
        tsum[0:MAIN, s] = main_total(ab, xl) + land3[ab].astype(F32)

    teach = tsum[...]
    mean_own = jnp.mean(teach, axis=-1, keepdims=True)
    cent = teach - mean_own
    m2_own = jnp.sum(cent * cent, axis=-1, keepdims=True)
    lane = lax.broadcasted_iota(jnp.int32, (160, 128), 1)
    tpad[0:160, :] = jnp.where(lane == 0, mean_own, jnp.where(lane == 1, m2_own, 0.0))
    stat[0] = tpad[...].T[0:8, :]
    sc = [send(stat.at[0], stat.at[k], dev_y(k)) for k in (2, 1, 3)]

    for w in ft_c:
        w.wait_recv()
    for q in range(4):
        fwide[OWN * q : OWN * q + OWN, :] = unpack(feat_r[q])
    feats = fwide[...].astype(BF16)
    wc_c[1].wait_recv()
    pred[...] = dot_nt(feats, hk[...].reshape(768, 1024))
    for w in sc:
        w.wait_recv()
    means = [stat[k, 0:1, :] for k in range(4)]
    mean_row = (means[0] + means[1] + means[2] + means[3]) * 0.25
    m2_row = sum(stat[k, 1:2, :] for k in range(4)) + 768.0 * sum((m - mean_row) ** 2 for m in means)
    rpad[0:1, :] = mean_row
    rpad[1:2, :] = lax.rsqrt(m2_row * (1.0 / 3072) + EPS)
    cols = rpad[...].T
    mean_col, istd_col = cols[0:160, 0:1], cols[0:160, 1:2]
    for half in range(2):
        s = slice(384 * half, 384 * half + 384)
        target = ((tsum[:, s] - mean_col) * istd_col * tgain[half, y]).astype(BF16)
        grad[:, s] = ((pred[:, s] - target.astype(F32)) * SCALE).astype(BF16)

    grads = grad[...]
    fg[...] = dot(grads, hk[...].reshape(768, 1024)).reshape(4, OWN, 1024)
    for k in (2, 1, 3):
        fg_s[k - 1] = pack(fg[(y + k) % 4])
    fg_c = [send(fg_s.at[k - 1], fg_r.at[k - 1], dev_y(k)) for k in (2, 1, 3)]

    hgt = dot_tn(grads, feats).astype(BF16)
    for half in range(2):
        hx[half] = hgt[:, 512 * half : 512 * half + 512].reshape(2, 4, 96, 512)

    def core_out(xbuf, crbuf):
        return send(xbuf.at[1 - c], crbuf, other)

    def z_out(xbuf, crbuf, ybuf, yown, zrbuf, arrival):
        arrival.wait_recv()
        out = []
        for k in (2, 1, 3, 0):
            q = (z + k) % 4
            value = xbuf[c, :, q].astype(F32) + crbuf[:, q].astype(F32)
            if k == 0:
                yown[...] = value
            else:
                ybuf[k - 1] = value.astype(BF16)
                out.append(send(ybuf.at[k - 1], zrbuf.at[k - 1], dev_z(k)))
        return out

    def x_out(yown, zrbuf, zbuf, xrbuf, arrivals):
        for w in arrivals:
            w.wait_recv()
        value = yown[...] + zrbuf[0].astype(F32) + zrbuf[1].astype(F32) + zrbuf[2].astype(F32)
        zbuf[...] = value.astype(BF16)
        out = [
            send(zbuf.at[1 - xl if k % 2 else xl], xrbuf.at[xx], dev_x(k)) for k in (2, 1, 3)
        ]
        xrbuf[xx] = zbuf[xl]
        return out

    def last(xrbuf, fin, arrivals):
        for w in arrivals:
            w.wait_recv()
        fin[c] = (xrbuf[0].astype(F32) + xrbuf[1].astype(F32)) + (xrbuf[2].astype(F32) + xrbuf[3].astype(F32))
        return send(fin.at[c], fin.at[c], other)

    hc_c = core_out(hx, hcr)

    hzc = z_out(hx, hcr, hy, hyo, hzr, hc_c)

    gsum = fg[y]
    for w in fg_c:
        w.wait_recv()
    for k in range(3):
        gsum = gsum + unpack(fg_r[k])
    weighted = gsum * sgain[...]
    nrm = normed_v[...]
    first = jnp.mean(weighted, axis=-1, keepdims=True)
    second = jnp.mean(weighted * nrm, axis=-1, keepdims=True)
    sg_s[...] = pack(istd_v[:, 0:1] * (weighted - first - nrm * second))
    sg_c = [send(sg_s, sg_r.at[y], dev_y(k)) for k in (2, 1, 3)]
    sg_r[y] = sg_s[...]

    for w in sg_c:
        w.wait_recv()
    for q in range(4):
        sgw[OWN * q : OWN * q + OWN, :] = unpack(sg_r[q])
    sgrads = sgw[...].astype(BF16)
    pbufs = (
        (px0, pcr0, py0, pyo0, pzr0, pz0, pxr0),
        (px1, pcr1, py1, pyo1, pzr1, pz1, pxr1),
    )
    pc_c = []
    for layer in range(2):
        px = pbufs[layer][0]
        for half in range(2):
            j = 2 * layer + half
            block = ctx_f[:, 128 * j : 128 * j + 128].astype(BF16)
            value = dot_tn(block, sgrads).astype(BF16)
            for s in range(2):
                px[s, half] = value[:, 512 * s : 512 * s + 512].reshape(4, 32, 512)
        pc_c.append(core_out(px, pbufs[layer][1]))
    pzc = []
    for layer in range(2):
        px, pcr, py, pyo, pzr, pz, pxr = pbufs[layer]
        pzc.append(z_out(px, pcr, py, pyo, pzr, pc_c[layer]))
    hxc = x_out(hyo, hzr, hz, hxr, hzc)
    pxc = []
    for layer in range(2):
        px, pcr, py, pyo, pzr, pz, pxr = pbufs[layer]
        pxc.append(x_out(pyo, pzr, pz, pxr, pzc[layer]))
    hlast = last(hxr, hfin, hxc)
    plast = [last(pbufs[layer][6], pfin.at[layer], pxc[layer]) for layer in range(2)]
    hlast.wait_recv()
    for s in range(2):
        hg_out[:, 512 * s : 512 * s + 512] = hfin[s]
    for layer in range(2):
        plast[layer].wait_recv()
        for s in range(2):
            pg_out[layer, :, 512 * s : 512 * s + 512] = pfin[layer, s]
    for copy in copies:
        copy.wait_send()

    @pl.when(jnp.logical_not(strm_self))
    def _():
        strm_to.wait_send()

    for mine, copy in ctx_to:

        @pl.when(jnp.logical_not(mine))
        def _():
            copy.wait_send()

    assert slots[0] <= N_SLOTS


N_SLOTS = 128


def emit(hg_in, pg_in, hg_out, pg_out, sem):
    copies = [
        pltpu.make_async_copy(hg_in, hg_out, sem.at[0]),
        pltpu.make_async_copy(pg_in, pg_out, sem.at[1]),
    ]
    for copy in copies:
        copy.start()
    for copy in copies:
        copy.wait()


def per_device(
    teacher_hidden, teacher_down, teacher_gain, student_stream, contexts, proj_weight, student_gain, head_weight
):
    vmem = pl.BlockSpec(memory_space=pltpu.VMEM)
    hbm = pl.BlockSpec(memory_space=pl.ANY)

    def v(*shape, dtype=BF16):
        return pltpu.VMEM(shape, dtype)

    def reduce_bufs(tail):
        return [
            v(2, 2, 4, *tail), v(2, 4, *tail), v(3, 2, *tail), v(2, *tail, dtype=F32),
            v(3, 2, *tail), v(2, *tail), v(4, *tail),
        ]

    def ring_bufs(rows):
        return [v(2, 3, 4, rows, 384), v(2, 4, rows, 384, dtype=F32), v(2, 2, 4, rows, 384), v(2, 2, 4, rows, 384)]

    scratch = [
        v(4, 2, MAIN, 768), v(2, 4, SIDE, 768), v(4, 768, 384), v(768, 1536),
        *ring_bufs(2 * MAIN),
        v(2, 3, 2, MAIN, 384), v(2, 2, MAIN, 384, dtype=F32), v(2, 2, 2, MAIN, 384), v(2, 2, 2, MAIN, 384),
        *ring_bufs(SIDE),
        v(2, 3, SIDE, 384), v(2, SIDE, 384, dtype=F32), v(2, 3, SIDE, 384),
        v(2, 4, 4, SIDE, 384), v(2, 4, 4, SIDE, 384), v(2, 4, 4, SIDE, 384, dtype=F32),
        v(2, MAIN, 384), v(2, MAIN, 384),
        v(160, 768, dtype=F32),
        v(80, 512), v(80, 512), v(4, 160, 128), v(4, 160, 128), v(160, 512, dtype=F32),
        v(2, 2, 4, 32, 1024), v(2, 4, 96, 1024),
        v(3, 80, 512), v(3, 80, 512), v(80, 512), v(4, 80, 512), v(160, 1024, dtype=F32),
        v(OWN, 1024, dtype=F32), v(OWN, 128, dtype=F32), v(160, 768, dtype=F32),
        v(256, 128, dtype=F32), v(4, 8, 256, dtype=F32), v(128, 256, dtype=F32), v(160, 768),
        v(4, OWN, 1024, dtype=F32), v(3, 80, 512), v(3, 80, 512), v(80, 512), v(4, 80, 512),
        v(160, 1024, dtype=F32),
        *reduce_bufs((96, 512)),
        *reduce_bufs((32, 512)),
        *reduce_bufs((32, 512)),
        v(2, 96, 512, dtype=F32), v(2, 2, 32, 512, dtype=F32),
        pltpu.SemaphoreType.DMA((16,)), pltpu.SemaphoreType.DMA((N_SLOTS,)), pltpu.SemaphoreType.DMA((N_SLOTS,)),
        pltpu.SemaphoreType.DMA((4,)), pltpu.SemaphoreType.DMA((10,)),
    ]
    head_grad, proj_grad = pl.pallas_call(
        kernel,
        out_shape=(
            jax.ShapeDtypeStruct((96, 1024), F32),
            jax.ShapeDtypeStruct((2, 32, 1024), F32),
        ),
        in_specs=[hbm, hbm, vmem, vmem, vmem, hbm, vmem, hbm],
        out_specs=(vmem, vmem),
        scratch_shapes=scratch,
        compiler_params=pltpu.CompilerParams(
            collective_id=0, has_side_effects=True, vmem_limit_bytes=56 * 2**20
        ),
        cost_estimate=pl.CostEstimate(flops=6 * 10**9, bytes_accessed=8 * 10**6, transcendentals=0),
    )(
        teacher_hidden.reshape(8, 160, 768),
        teacher_down,
        teacher_gain.reshape(2, 4, 1, 384),
        student_stream,
        contexts,
        proj_weight,
        student_gain.reshape(1, 1024),
        head_weight.T,
    )
    head_grad, proj_grad = pl.pallas_call(
        emit,
        out_shape=(
            jax.ShapeDtypeStruct((96, 1024), F32),
            jax.ShapeDtypeStruct((2, 32, 1024), F32),
        ),
        in_specs=[vmem, vmem],
        out_specs=(hbm, hbm),
        scratch_shapes=[pltpu.SemaphoreType.DMA((2,))],
    )(head_grad, proj_grad)
    return head_grad.T, proj_grad


def solution(mesh):
    in_specs = (
        P("dp", "tensor"),
        P("tensor", None),
        P(),
        P(("dp", "tensor"), None),
        P(None, ("dp", "tensor"), None),
        P(None, "tensor", None),
        P(),
        P(None, "tensor"),
    )
    out_specs = (P(None, "tensor"), P(None, "tensor", None))
    return jax.shard_map(
        per_device, mesh=mesh, in_specs=in_specs, out_specs=out_specs, check_vma=False
    )
```

```python
import functools
import math

import jax
import jax.numpy as jnp
from jax import lax
from jax.experimental import pallas as pl
from jax.experimental.pallas import tpu as pltpu
from jax.sharding import PartitionSpec as P

MESH = pl.DeviceIdType.MESH
F32 = jnp.float32
BF16 = jnp.bfloat16
EPS = 1e-06
OWN = 40
SIDE = 64
MAIN = 160 - SIDE
SCALE = 1.0 / math.sqrt(5120)


def dot(a, b):
    return jnp.dot(a, b, preferred_element_type=F32)


def dot_nt(a, b):
    return lax.dot_general(a, b, (((1,), (1,)), ((), ())), preferred_element_type=F32)


def pack(v):
    return jnp.concatenate([v[:, 0:512], v[:, 512:1024]], axis=0).astype(BF16)


def unpack(b):
    v = b.astype(F32)
    return jnp.concatenate([v[0:OWN], v[OWN : 2 * OWN]], axis=1)


def dot_tn(a, b):
    return lax.dot_general(a, b, (((0,), (0,)), ((), ())), preferred_element_type=F32)


def kernel(
    hid, down, tgain, stream_in, ctx, pw, sgain, headt,
    hg_out, pg_out,
    hm_v, hs_v, down_v, down_b,
    msend1, mown1, mrly1, mland1, msend2, mown2, mrly2, mland2,
    ssend1, sown1, srly1, sland1, ssend2, sown2, sland2,
    xs, xr, xown,
    send3, land3,
    tsum,
    strm_s, strm_r, ctx_s, ctx_r, ctx_f,
    wk, hk,
    st_s, st_r, feat_s, feat_r, fwide,
    normed_v, istd_v, pred,
    tpad, stat, rpad, grad,
    fg, fg_s, fg_r, sg_s, sg_r, sgw,
    hx, hcr, hy, hyo, hzr, hz, hxr,
    px0, pcr0, py0, pyo0, pzr0, pz0, pxr0,
    px1, pcr1, py1, pyo1, pzr1, pz1, pxr1,
    hfin, pfin,
    lsem, ssem, rsem, tsem, usem,
):
    dp = lax.axis_index("dp")
    t = lax.axis_index("tensor")
    h, c = dp // 2, dp % 2
    xl, y, z = t // 16, (t // 4) % 4, t % 4
    xx = 2 * h + xl

    def dev(h_, c_, xl_, y_, z_):
        return {"dp": h_ * 2 + c_, "tensor": xl_ * 16 + y_ * 4 + z_}

    def dev_y(k):
        return dev(h, c, xl, (y + k) % 4, z)

    def dev_z(k):
        return dev(h, c, xl, y, (z + k) % 4)

    def dev_x(k):
        n = (xx + k) % 4
        return dev(n // 2, c, n % 2, y, z)

    xlo = dev(h, c, 1 - xl, y, z)
    xhi = dev(1 - h, c, 1 - xl, y, z)
    other = dev(h, 1 - c, xl, y, z)

    slots = [0]
    copies = []

    def send(src, dst, to):
        i = slots[0]
        slots[0] += 1
        copy = pltpu.make_async_remote_copy(
            src_ref=src, dst_ref=dst, send_sem=ssem.at[i], recv_sem=rsem.at[i],
            device_id=to, device_id_type=MESH,
        )
        copy.start()
        copies.append(copy)
        return copy

    loads = []

    def load(src, dst):
        copy = pltpu.make_async_copy(src, dst, lsem.at[len(loads)])
        copy.start()
        loads.append(copy)

    def dcol(q):
        return down.at[:, pl.ds(pl.multiple_of(384 * q, 128), 384)]

    lanes = pl.ds(pl.multiple_of(512 * c, 128), 512)
    for half in range(2):
        load(hid.at[pl.ds(4 * half, 4), pl.ds(0, MAIN)], hm_v.at[:, half])
    load(dcol((y + 2) % 4), down_v.at[2])
    load(down.at[:, pl.ds(1536, 1536)], down_b)
    for half in range(2):
        load(hid.at[pl.ds(4 * half, 4), pl.ds(MAIN, SIDE)], hs_v.at[half])
    load(pw.at[:, :, lanes], wk.at[:, xl, z, :, lanes])
    load(headt.at[:, lanes], hk.at[xl, z, :, lanes])
    for k in (1, 3, 0):
        load(dcol((y + k) % 4), down_v.at[k])

    barrier = pltpu.get_barrier_semaphore()
    for to in (
        [dev_y(k) for k in (1, 2, 3)] + [dev_z(k) for k in (1, 2, 3)]
        + [dev_x(k) for k in (1, 2, 3)] + [other]
    ):
        pl.semaphore_signal(barrier, 1, device_id=to, device_id_type=MESH)
    for j in range(4):
        mine = jnp.where(jnp.logical_and(y == z, z == j), 1, 0)
        to = dev(h, c + mine * (1 - 2 * c), xl, z, j)
        pl.semaphore_signal(barrier, 1, device_id=to, device_id_type=MESH)

    tpad[...] = jnp.zeros_like(tpad)
    rpad[...] = jnp.zeros_like(rpad)

    def main_product(ab, k):
        if ab == 0:
            value = dot(hm_v[...].reshape(8 * MAIN, 768), down_v[k]).reshape(4, 2 * MAIN, 384)
            if k == 0:
                mown1[0] = value
            else:
                msend1[0, k - 1] = value.astype(BF16)
            return

        value = dot(hm_v[(z + k) % 4].reshape(2 * MAIN, 768), down_b[...])
        for i in range(4):
            block = value[:, 384 * i : 384 * i + 384]
            if k == 0:
                mown1[1, i] = block
            else:
                msend1[1, k - 1, i] = block.astype(BF16)

    def side_product_y(k, rows, out):
        out[0, k] = dot(hs_v[rows].reshape(4 * SIDE, 768), down_v[k]).reshape(4, SIDE, 384).astype(out.dtype)

    def side_product_z(rows, out):
        value = dot(hs_v[rows].reshape(4 * SIDE, 768), down_b[...]).reshape(4, SIDE, 1536).astype(out.dtype)
        for q in range(4):
            for i in range(4):
                out[1, (q - z + 4) % 4, i] = value[q, :, 384 * i : 384 * i + 384]

    class Ring:
        def __init__(self, to, ab, n, sbuf, rly, land):
            self.to, self.ab, self.n, self.m = to, ab, n, n // 2
            self.sbuf, self.rly, self.land = sbuf, rly, land
            self.relays, self.final = [], []

        def halves(self):
            return pl.ds(0, self.m), pl.ds(self.m, self.n - self.m)

        def relay_out(self):
            low, high = self.halves()
            for d, part in ((0, low), (1, high)):
                self.relays.append(
                    send(self.sbuf.at[self.ab, 1, part], self.rly.at[self.ab, d, part], self.to(1 + 2 * d))
                )

        def direct_out(self, k):
            low, high = self.halves()
            d, part = (0, high) if k == 1 else (1, low)
            self.final.append(
                send(self.sbuf.at[self.ab, k - 1, part], self.land.at[self.ab, d, part], self.to(k))
            )

        def relay_on(self):
            low, high = self.halves()
            for d, k, part, slabs in (
                (0, 1, low, range(self.m)),
                (1, 3, high, range(self.m, self.n)),
            ):
                self.relays[d].wait_recv()
                for i in slabs:
                    value = self.sbuf[self.ab, k - 1, i].astype(F32) + self.rly[self.ab, d, i].astype(F32)
                    self.sbuf[self.ab, k - 1, i] = value.astype(BF16)
                self.final.append(
                    send(self.sbuf.at[self.ab, k - 1, part], self.land.at[self.ab, d, part], self.to(k))
                )

        def finish(self):
            for w in self.final:
                w.wait_recv()

    main1 = [Ring(dev_y, 0, 4, msend1, mrly1, mland1), Ring(dev_z, 1, 4, msend1, mrly1, mland1)]
    main2 = [Ring(dev_z, 0, 2, msend2, mrly2, mland2), Ring(dev_y, 1, 2, msend2, mrly2, mland2)]
    side1 = [Ring(dev_y, 0, 4, ssend1, srly1, sland1), Ring(dev_z, 1, 4, ssend1, srly1, sland1)]

    strm_s[...] = pack(stream_in[...].astype(F32))
    for q in range(4):
        parts = [
            ctx[layer, :, 512 * half + 128 * q : 512 * half + 128 * q + 128].astype(F32)
            for layer in range(2)
            for half in range(2)
        ]
        ctx_s[q] = jnp.concatenate(parts, axis=0).astype(BF16)
    pl.semaphore_wait(barrier, 14)
    strm_self = jnp.logical_and(y == z, z == y)
    strm_to = pltpu.make_async_remote_copy(
        src_ref=strm_s, dst_ref=strm_r, send_sem=usem.at[8], recv_sem=usem.at[9],
        device_id=dev(h, c, xl, z, y), device_id_type=MESH,
    )

    @pl.when(strm_self)
    def _():
        pltpu.make_async_copy(strm_s, strm_r, usem.at[9]).start()

    @pl.when(jnp.logical_not(strm_self))
    def _():
        strm_to.start()

    ctx_to = []
    for q in range(4):
        mine = jnp.logical_and(y == z, y == q)
        copy = pltpu.make_async_remote_copy(
            src_ref=ctx_s.at[q], dst_ref=ctx_r.at[z], send_sem=usem.at[q], recv_sem=tsem.at[z],
            device_id=dev(h, c, xl, q, y), device_id_type=MESH,
        )
        ctx_to.append((mine, copy))

        @pl.when(mine)
        def _():
            pltpu.make_async_copy(ctx_s.at[q], ctx_r.at[z], tsem.at[z]).start()

        @pl.when(jnp.logical_not(mine))
        def _():
            copy.start()

    loads[6].wait()
    wz_c = [send(wk.at[:, xl, z, :, lanes], wk.at[:, xl, z, :, lanes], dev_z(k)) for k in (2, 1, 3)]
    for i in range(3):
        loads[i].wait()
    main_product(0, 2)
    main1[0].relay_out()
    for i in range(3, 6):
        loads[i].wait()
    main_product(1, 2)
    main1[1].relay_out()
    loads[7].wait()
    hz_c = [send(hk.at[xl, z, :, lanes], hk.at[xl, z, :, lanes], dev_z(k)) for k in (2, 1, 3)]
    xc = [[None] * 4, [None] * 4]

    def x_first(ab, k):
        xc[ab][k] = send(xs.at[ab, k], xr.at[ab, k], xlo)

    side_product_y(2, 1 - xl, xs)
    x_first(0, 2)

    side_product_z(1 - xl, xs)
    x_first(1, 2)
    for i in range(8, 11):
        loads[i].wait()
    for ab in range(2):
        for k in (1, 3):
            main_product(ab, k)
            main1[ab].direct_out(k)
    for k in (1, 3, 0):
        side_product_y(k, 1 - xl, xs)
        x_first(0, k)
        x_first(1, k)
    for w in wz_c:
        w.wait_recv()
    wx_c = [send(wk.at[:, xl, :, :, lanes], wk.at[:, xl, :, :, lanes], xhi)]
    main_product(0, 0)
    main_product(1, 0)
    for k in (2, 1, 3, 0):
        side_product_y(k, xl, xown)
    side_product_z(xl, xown)
    for ab in range(2):
        main1[ab].relay_on()

    def side_add(ab, k):
        xc[ab][k].wait_recv()
        value = xown[ab, k] + xr[ab, k].astype(F32)
        if k == 0:
            sown1[ab] = value
        else:
            ssend1[ab, k - 1] = value.astype(BF16)

    for ab in range(2):
        side_add(ab, 2)
        side1[ab].relay_out()
    for j in range(4):
        pltpu.make_async_remote_copy(
            src_ref=ctx_s.at[j], dst_ref=ctx_r.at[j], send_sem=usem.at[j], recv_sem=tsem.at[j],
            device_id=dev(h, c, xl, j, y), device_id_type=MESH,
        ).wait_recv()
        block = ctx_r[j].astype(F32)
        for i in range(4):
            ctx_f[OWN * j : OWN * j + OWN, 128 * i : 128 * i + 128] = block[OWN * i : OWN * i + OWN]
    wx_c[0].wait_recv()
    wc_c = [send(wk.at[:, :, :, :, lanes], wk.at[:, :, :, :, lanes], other)]
    wc_c[0].wait_recv()
    fg[...] = dot(ctx_f[...].astype(BF16), wk[...].reshape(512, 1024)).reshape(4, OWN, 1024)
    for k in (2, 1, 3):
        st_s[k - 1] = pack(fg[(y + k) % 4])
    st_c = [send(st_s.at[k - 1], st_r.at[k - 1], dev_y(k)) for k in (2, 1, 3)]
    for w in hz_c:
        w.wait_recv()
    wx_c.append(send(hk.at[xl, :, :, lanes], hk.at[xl, :, :, lanes], xhi))
    for ab in range(2):
        side_add(ab, 1)
        side1[ab].direct_out(1)


    def total1(own1, land1, ab, k):
        q = ((z if ab == 0 else y) + k) % 4
        return own1[ab, q] + land1[ab, 0, q].astype(F32) + land1[ab, 1, q].astype(F32)

    def main_second(ab):
        main1[ab].finish()
        for k in (2, 1, 3, 0):
            value = total1(mown1, mland1, ab, k).reshape(2, MAIN, 384)
            if k == 0:
                mown2[ab] = value
                continue
            msend2[ab, k - 1] = value.astype(BF16)
            if k == 2:
                main2[ab].relay_out()
            else:
                main2[ab].direct_out(k)

    def side_second(ab):
        side1[ab].finish()
        out = []
        for k in (2, 1, 3, 0):
            value = total1(sown1, sland1, ab, k)
            if k == 0:
                sown2[ab] = value
                continue
            ssend2[ab, k - 1] = value.astype(BF16)
            to = dev_z(k) if ab == 0 else dev_y(k)
            out.append(send(ssend2.at[ab, k - 1], sland2.at[ab, k - 1], to))
        return out

    side_add(0, 3)
    side1[0].direct_out(3)
    side1[0].relay_on()
    main_second(0)
    side_add(1, 3)
    side1[1].direct_out(3)
    side1[1].relay_on()
    main_second(1)
    strm_to.wait_recv()
    stream = unpack(strm_r[...]) + fg[y]
    for w in st_c:
        w.wait_recv()
    for k in range(3):
        stream = stream + unpack(st_r[k])
    centered = stream - jnp.mean(stream, axis=-1, keepdims=True)
    istd = lax.rsqrt(jnp.mean(centered * centered, axis=-1, keepdims=True) + EPS)
    normed = centered * istd
    normed_v[...] = normed
    istd_v[...] = jnp.broadcast_to(istd, istd_v.shape)
    feat_s[...] = pack(normed * sgain[...])
    ft_c = [send(feat_s, feat_r.at[y], dev_y(k)) for k in (2, 1, 3)]
    feat_r[y] = feat_s[...]
    wx_c[1].wait_recv()
    wc_c.append(send(hk.at[:, :, :, lanes], hk.at[:, :, :, lanes], other))
    main2[0].relay_on()
    main2[1].relay_on()
    side2 = []
    for ab in range(2):
        side_add(ab, 0)
        side2.append(side_second(ab))
    def main_total(ab, q):
        return mown2[ab, q] + mland2[ab, 0, q].astype(F32) + mland2[ab, 1, q].astype(F32)

    x3 = []
    for ab in range(2):
        main2[ab].finish()
        send3[ab] = main_total(ab, 1 - xl).astype(BF16)
        x3.append(send(send3.at[ab], land3.at[ab], xlo))


    for ab in range(2):
        s = slice(384 * ab, 384 * ab + 384)
        for w in side2[ab]:
            w.wait_recv()
        value = sown2[ab]
        for k in range(3):
            value = value + sland2[ab, k].astype(F32)
        tsum[MAIN:160, s] = value
        x3[ab].wait_recv()
        tsum[0:MAIN, s] = main_total(ab, xl) + land3[ab].astype(F32)

    teach = tsum[...]
    mean_own = jnp.mean(teach, axis=-1, keepdims=True)
    cent = teach - mean_own
    m2_own = jnp.sum(cent * cent, axis=-1, keepdims=True)
    lane = lax.broadcasted_iota(jnp.int32, (160, 128), 1)
    tpad[0:160, :] = jnp.where(lane == 0, mean_own, jnp.where(lane == 1, m2_own, 0.0))
    stat[0] = tpad[...].T[0:8, :]
    sc = [send(stat.at[0], stat.at[k], dev_y(k)) for k in (2, 1, 3)]

    for w in ft_c:
        w.wait_recv()
    for q in range(4):
        fwide[OWN * q : OWN * q + OWN, :] = unpack(feat_r[q])
    feats = fwide[...].astype(BF16)
    wc_c[1].wait_recv()
    pred[...] = dot_nt(feats, hk[...].reshape(768, 1024))
    for w in sc:
        w.wait_recv()
    means = [stat[k, 0:1, :] for k in range(4)]
    mean_row = (means[0] + means[1] + means[2] + means[3]) * 0.25
    m2_row = sum(stat[k, 1:2, :] for k in range(4)) + 768.0 * sum((m - mean_row) ** 2 for m in means)
    rpad[0:1, :] = mean_row
    rpad[1:2, :] = lax.rsqrt(m2_row * (1.0 / 3072) + EPS)
    cols = rpad[...].T
    mean_col, istd_col = cols[0:160, 0:1], cols[0:160, 1:2]
    for half in range(2):
        s = slice(384 * half, 384 * half + 384)
        target = ((tsum[:, s] - mean_col) * istd_col * tgain[half, y]).astype(BF16)
        grad[:, s] = ((pred[:, s] - target.astype(F32)) * SCALE).astype(BF16)

    grads = grad[...]
    fg[...] = dot(grads, hk[...].reshape(768, 1024)).reshape(4, OWN, 1024)
    for k in (2, 1, 3):
        fg_s[k - 1] = pack(fg[(y + k) % 4])
    fg_c = [send(fg_s.at[k - 1], fg_r.at[k - 1], dev_y(k)) for k in (2, 1, 3)]

    hgt = dot_tn(grads, feats).astype(BF16)
    for half in range(2):
        hx[half] = hgt[:, 512 * half : 512 * half + 512].reshape(2, 4, 96, 512)

    def core_out(xbuf, crbuf):
        return send(xbuf.at[1 - c], crbuf, other)

    def z_out(xbuf, crbuf, ybuf, yown, zrbuf, arrival):
        arrival.wait_recv()
        out = []
        for k in (2, 1, 3, 0):
            q = (z + k) % 4
            value = xbuf[c, :, q].astype(F32) + crbuf[:, q].astype(F32)
            if k == 0:
                yown[...] = value
            else:
                ybuf[k - 1] = value.astype(BF16)
                out.append(send(ybuf.at[k - 1], zrbuf.at[k - 1], dev_z(k)))
        return out

    def x_out(yown, zrbuf, zbuf, xrbuf, arrivals):
        for w in arrivals:
            w.wait_recv()
        value = yown[...] + zrbuf[0].astype(F32) + zrbuf[1].astype(F32) + zrbuf[2].astype(F32)
        zbuf[...] = value.astype(BF16)
        out = [
            send(zbuf.at[1 - xl if k % 2 else xl], xrbuf.at[xx], dev_x(k)) for k in (2, 1, 3)
        ]
        xrbuf[xx] = zbuf[xl]
        return out

    def last(xrbuf, fin, arrivals):
        for w in arrivals:
            w.wait_recv()
        fin[c] = (xrbuf[0].astype(F32) + xrbuf[1].astype(F32)) + (xrbuf[2].astype(F32) + xrbuf[3].astype(F32))
        return send(fin.at[c], fin.at[c], other)

    hc_c = core_out(hx, hcr)

    hzc = z_out(hx, hcr, hy, hyo, hzr, hc_c)

    gsum = fg[y]
    for w in fg_c:
        w.wait_recv()
    for k in range(3):
        gsum = gsum + unpack(fg_r[k])
    weighted = gsum * sgain[...]
    nrm = normed_v[...]
    first = jnp.mean(weighted, axis=-1, keepdims=True)
    second = jnp.mean(weighted * nrm, axis=-1, keepdims=True)
    sg_s[...] = pack(istd_v[:, 0:1] * (weighted - first - nrm * second))
    sg_c = [send(sg_s, sg_r.at[y], dev_y(k)) for k in (2, 1, 3)]
    sg_r[y] = sg_s[...]

    for w in sg_c:
        w.wait_recv()
    for q in range(4):
        sgw[OWN * q : OWN * q + OWN, :] = unpack(sg_r[q])
    sgrads = sgw[...].astype(BF16)
    pbufs = (
        (px0, pcr0, py0, pyo0, pzr0, pz0, pxr0),
        (px1, pcr1, py1, pyo1, pzr1, pz1, pxr1),
    )
    pc_c = []
    for layer in range(2):
        px = pbufs[layer][0]
        for half in range(2):
            j = 2 * layer + half
            block = ctx_f[:, 128 * j : 128 * j + 128].astype(BF16)
            value = dot_tn(block, sgrads).astype(BF16)
            for s in range(2):
                px[s, half] = value[:, 512 * s : 512 * s + 512].reshape(4, 32, 512)
        pc_c.append(core_out(px, pbufs[layer][1]))
    pzc = []
    for layer in range(2):
        px, pcr, py, pyo, pzr, pz, pxr = pbufs[layer]
        pzc.append(z_out(px, pcr, py, pyo, pzr, pc_c[layer]))
        if layer == 0:
            hxc = x_out(hyo, hzr, hz, hxr, hzc)
    pxc = []
    for layer in range(2):
        px, pcr, py, pyo, pzr, pz, pxr = pbufs[layer]
        pxc.append(x_out(pyo, pzr, pz, pxr, pzc[layer]))
    hlast = last(hxr, hfin, hxc)
    plast = [last(pbufs[layer][6], pfin.at[layer], pxc[layer]) for layer in range(2)]
    hlast.wait_recv()
    for s in range(2):
        hg_out[:, 512 * s : 512 * s + 512] = hfin[s]
    for layer in range(2):
        plast[layer].wait_recv()
        for s in range(2):
            pg_out[layer, :, 512 * s : 512 * s + 512] = pfin[layer, s]
    for copy in copies:
        copy.wait_send()

    @pl.when(jnp.logical_not(strm_self))
    def _():
        strm_to.wait_send()

    for mine, copy in ctx_to:

        @pl.when(jnp.logical_not(mine))
        def _():
            copy.wait_send()

    assert slots[0] <= N_SLOTS


N_SLOTS = 128


def emit(hg_in, pg_in, hg_out, pg_out, sem):
    copies = [
        pltpu.make_async_copy(hg_in, hg_out, sem.at[0]),
        pltpu.make_async_copy(pg_in, pg_out, sem.at[1]),
    ]
    for copy in copies:
        copy.start()
    for copy in copies:
        copy.wait()


def per_device(
    teacher_hidden, teacher_down, teacher_gain, student_stream, contexts, proj_weight, student_gain, head_weight
):
    vmem = pl.BlockSpec(memory_space=pltpu.VMEM)
    hbm = pl.BlockSpec(memory_space=pl.ANY)

    def v(*shape, dtype=BF16):
        return pltpu.VMEM(shape, dtype)

    def reduce_bufs(tail):
        return [
            v(2, 2, 4, *tail), v(2, 4, *tail), v(3, 2, *tail), v(2, *tail, dtype=F32),
            v(3, 2, *tail), v(2, *tail), v(4, *tail),
        ]

    def ring_bufs(rows):
        return [v(2, 3, 4, rows, 384), v(2, 4, rows, 384, dtype=F32), v(2, 2, 4, rows, 384), v(2, 2, 4, rows, 384)]

    scratch = [
        v(4, 2, MAIN, 768), v(2, 4, SIDE, 768), v(4, 768, 384), v(768, 1536),
        *ring_bufs(2 * MAIN),
        v(2, 3, 2, MAIN, 384), v(2, 2, MAIN, 384, dtype=F32), v(2, 2, 2, MAIN, 384), v(2, 2, 2, MAIN, 384),
        *ring_bufs(SIDE),
        v(2, 3, SIDE, 384), v(2, SIDE, 384, dtype=F32), v(2, 3, SIDE, 384),
        v(2, 4, 4, SIDE, 384), v(2, 4, 4, SIDE, 384), v(2, 4, 4, SIDE, 384, dtype=F32),
        v(2, MAIN, 384), v(2, MAIN, 384),
        v(160, 768, dtype=F32),
        v(80, 512), v(80, 512), v(4, 160, 128), v(4, 160, 128), v(160, 512, dtype=F32),
        v(2, 2, 4, 32, 1024), v(2, 4, 96, 1024),
        v(3, 80, 512), v(3, 80, 512), v(80, 512), v(4, 80, 512), v(160, 1024, dtype=F32),
        v(OWN, 1024, dtype=F32), v(OWN, 128, dtype=F32), v(160, 768, dtype=F32),
        v(256, 128, dtype=F32), v(4, 8, 256, dtype=F32), v(128, 256, dtype=F32), v(160, 768),
        v(4, OWN, 1024, dtype=F32), v(3, 80, 512), v(3, 80, 512), v(80, 512), v(4, 80, 512),
        v(160, 1024, dtype=F32),
        *reduce_bufs((96, 512)),
        *reduce_bufs((32, 512)),
        *reduce_bufs((32, 512)),
        v(2, 96, 512, dtype=F32), v(2, 2, 32, 512, dtype=F32),
        pltpu.SemaphoreType.DMA((16,)), pltpu.SemaphoreType.DMA((N_SLOTS,)), pltpu.SemaphoreType.DMA((N_SLOTS,)),
        pltpu.SemaphoreType.DMA((4,)), pltpu.SemaphoreType.DMA((10,)),
    ]
    head_grad, proj_grad = pl.pallas_call(
        kernel,
        out_shape=(
            jax.ShapeDtypeStruct((96, 1024), F32),
            jax.ShapeDtypeStruct((2, 32, 1024), F32),
        ),
        in_specs=[hbm, hbm, vmem, vmem, vmem, hbm, vmem, hbm],
        out_specs=(vmem, vmem),
        scratch_shapes=scratch,
        compiler_params=pltpu.CompilerParams(
            collective_id=0, has_side_effects=True, vmem_limit_bytes=56 * 2**20
        ),
        cost_estimate=pl.CostEstimate(flops=6 * 10**9, bytes_accessed=8 * 10**6, transcendentals=0),
    )(
        teacher_hidden.reshape(8, 160, 768),
        teacher_down,
        teacher_gain.reshape(2, 4, 1, 384),
        student_stream,
        contexts,
        proj_weight,
        student_gain.reshape(1, 1024),
        head_weight.T,
    )
    head_grad, proj_grad = pl.pallas_call(
        emit,
        out_shape=(
            jax.ShapeDtypeStruct((96, 1024), F32),
            jax.ShapeDtypeStruct((2, 32, 1024), F32),
        ),
        in_specs=[vmem, vmem],
        out_specs=(hbm, hbm),
        scratch_shapes=[pltpu.SemaphoreType.DMA((2,))],
    )(head_grad, proj_grad)
    return head_grad.T, proj_grad


def solution(mesh):
    in_specs = (
        P("dp", "tensor"),
        P("tensor", None),
        P(),
        P(("dp", "tensor"), None),
        P(None, ("dp", "tensor"), None),
        P(None, "tensor", None),
        P(),
        P(None, "tensor"),
    )
    out_specs = (P(None, "tensor"), P(None, "tensor", None))
    return jax.shard_map(
        per_device, mesh=mesh, in_specs=in_specs, out_specs=out_specs, check_vma=False
    )
```
